256 devices in a mesh: dyn: 16 (over x_lo, z), phys: 16 (over x_hi, y, core).
Axes of the slice: x: 4 (x_hi: 2, x_lo: 2; x = x_hi * 2 + x_lo), y: 4, z: 8, core: 2. Of those that a mesh axis runs over, the one named last changes fastest.
Arguments:
- initial_state: float32 [72, 256, 2048], P(None, ('dyn', 'phys')), may hold values from -6 to 6
- prev_tendency: float32 [72, 256, 2048], P(None, ('dyn', 'phys')), may hold values from -3 to 3
- analysis: float32 [72, 2, 256, 256], P(None, None, ('dyn', 'phys')), may hold values from -4 to 4
- legendre: float32 [256, 16, 16, 256], P('dyn', None, 'phys'), may hold values from -6 to 6
- nudge_rate: float32 [72], replicated, may hold values from 0.1 to 2
- band_waves: int32 [256], replicated, may hold values from 0 to 255, each once
- cloudy_count: int32 [4096], P(('dyn', 'phys')), may hold values from 1 to 128, as said below
- expert_of: int32 [4096, 1], P(('dyn', 'phys')), may hold values from 0 to 15, as said below
- w_in: bfloat16 [16, 72, 1024], P('phys'), may hold values from -0.75 to 0.75
- w_mid: bfloat16 [16, 1024, 1024], P('phys'), may hold values from -0.1875 to 0.1875
- w_out: bfloat16 [16, 72, 1024], P('phys'), may hold values from -0.1875 to 0.1875
Outputs:
- final_state: float32 [72, 256, 2048], P(None, ('dyn', 'phys'))
- tendency: bfloat16 [72, 256, 2048], P(None, ('dyn', 'phys'))
The draws below stay inside these ranges and needn't reach their ends.
Inputs may be any that keep to these rules, and one draw needn't show every extreme that they name: `band_waves`: each zonal wavenumber 0 .. 255 stands in exactly one slot. `cloudy_count`: some block of every device has 128 cloudy columns. `expert_of`: among the 16 blocks of one device no network is named more than 2 times; in every group of devices along phys one network is named exactly 2 times by each device of the group.
All inputs are finite; a program needn't handle non-finite values.
Results may differ from the reference program's by a relative error of at most 0.0065.
Values may be sent and summed in bfloat16 or wider, within the bound.
No kernel may reach another device: no remote copies, remote signals or barrier semaphores. Data moves between devices by JAX's collectives and lax.ppermute only.
A program may use at most 128 MiB of HBM per device.

```python
import math
import jax
import jax.numpy as jnp
from jax import lax

NLON = 2048
M = 256
K = 256
H = 1024
LEV = 72
STEPS = 2
NB_ROW = 16
CMAX = 128
LAT_DEV = 1
NLAT = 256
CAP = 2
N_DYN = 16
N_PHYS = 16


def draw_cloudy_count(key, part):
    key = jax.random.fold_in(key, 5)
    per_device = LAT_DEV * NB_ROW
    devices_all = NLAT // LAT_DEV
    counts = jax.random.randint(jax.random.fold_in(key, 1), (devices_all * per_device,), 1, CMAX + 1)
    chosen = jax.random.randint(jax.random.fold_in(key, 2), (devices_all,), 0, per_device)
    position = jnp.arange(devices_all * per_device, dtype=jnp.int32)
    full_mark = position % per_device == chosen[position // per_device]
    return jnp.where(full_mark, CMAX, counts).astype(jnp.int32)


def draw_expert_of(key, part):
    key = jax.random.fold_in(key, 7)
    per_device = LAT_DEV * NB_ROW
    devices_all = NLAT // LAT_DEV
    slot_total = N_PHYS * CAP
    heavy_row = jax.random.randint(jax.random.fold_in(key, 1), (devices_all // N_PHYS,), 0, N_PHYS)
    heavy = jnp.repeat(heavy_row, N_PHYS)
    device_keys = jax.random.split(jax.random.fold_in(key, 2), devices_all)

    def one_device(device_key, heavy_one):
        shuffled = jax.random.permutation(jax.random.fold_in(device_key, 1), slot_total)
        slot_ids = jnp.arange(slot_total, dtype=jnp.int32)
        rank_of = jnp.argsort(shuffled).astype(jnp.int32)
        score = jnp.where(slot_ids // CAP == heavy_one, slot_ids - slot_total, rank_of)
        picked = jnp.argsort(score)[:per_device]
        rows_out = jax.random.permutation(jax.random.fold_in(device_key, 2), picked)
        return rows_out // CAP
    experts = jax.vmap(one_device)(device_keys, heavy)
    return experts.reshape(devices_all * per_device, 1).astype(jnp.int32)


def shard_levels(key, extent, cuts, smallest, top_value):
    loudness = 1.0
    for axis_at, shards_of in cuts:
        steps = jax.random.uniform(jax.random.fold_in(jax.random.fold_in(key, 6), axis_at), (shards_of,), jnp.float32, smallest / len(cuts), top_value / len(cuts))
        loudness = loudness * jnp.repeat(jnp.exp(steps), extent[axis_at] // shards_of).reshape((-1,) + (1,) * (len(extent) - 1 - axis_at))
    return loudness


def bell_draw(key, extent, spread, most, pieces=(), kind=jnp.bfloat16):
    entries = jax.random.normal(key, extent, jnp.float32) * spread
    if len(pieces) > 0:
        entries = shard_levels(key, extent, pieces, -0.22, 0.18) * entries
    return jnp.clip(entries, min=-most, max=most).astype(kind)


def setup_inputs(seed: int = 0) -> dict:
    seeds = jax.random.split(jax.random.key(seed), 12)
    initial_state = bell_draw(seeds[0], (LEV, NLAT, NLON), 1.0, 6.0, ((1, 256),), jnp.float32)
    prev_tendency = bell_draw(seeds[1], (LEV, NLAT, NLON), 0.5, 3.0, ((1, 256),), jnp.float32)
    analysis = bell_draw(seeds[2], (LEV, 2, M, K), 0.5, 4.0, ((2, 256),), jnp.float32)
    legendre = bell_draw(seeds[3], (M, N_DYN, LAT_DEV * N_PHYS, K), 1.0, 6.0, ((0, 16), (2, 16)), jnp.float32)
    nudge_rate = jnp.clip(jnp.exp(jax.random.uniform(seeds[4], (LEV,), jnp.float32, math.log(0.1), math.log(2.0))), 0.1, 2.0)
    band_waves = jax.random.permutation(seeds[5], M).astype(jnp.int32)
    cloudy_count = draw_cloudy_count(jax.random.fold_in(seeds[11], 71), 0)
    expert_of = draw_expert_of(jax.random.fold_in(seeds[11], 71), 0)
    w_in = bell_draw(seeds[8], (N_PHYS, LEV, H), LEV ** -0.5, 0.75, ((0, 16),))
    w_mid = bell_draw(seeds[9], (N_PHYS, H, H), H ** -0.5, 0.1875, ((0, 16),))
    w_out = bell_draw(seeds[10], (N_PHYS, LEV, H), H ** -0.5, 0.1875, ((0, 16),))
    return {"initial_state": initial_state, "prev_tendency": prev_tendency, "analysis": analysis, "legendre": legendre, "nudge_rate": nudge_rate, "band_waves": band_waves, "cloudy_count": cloudy_count, "expert_of": expert_of, "w_in": w_in, "w_mid": w_mid, "w_out": w_out}


time_step = 0.5
diffusion = 1.0

def physics(initial_state, cloudy_count, expert_of, w_in, w_mid, w_out):
    levels = initial_state.shape[0]
    block_total = NLAT * NB_ROW
    segment_len = NLON // NB_ROW
    columns = initial_state.reshape(levels, block_total, segment_len)[:, :, :CMAX].astype(jnp.bfloat16)
    per_group = LAT_DEV * NB_ROW
    group_total = block_total // per_group
    grouped = jnp.transpose(columns.reshape(levels, group_total, per_group, CMAX), (1, 2, 0, 3))
    experts = expert_of[:, 0].reshape(group_total, per_group)

    def apply_group(group_pair):
        block_cols, block_experts = group_pair
        first_w = w_in[block_experts].astype(jnp.float32)
        middle_w = w_mid[block_experts].astype(jnp.float32)
        last_w = w_out[block_experts].astype(jnp.float32)
        hidden_one = jax.nn.silu(jnp.einsum('blc,blh->bhc', block_cols.astype(jnp.float32), first_w)).astype(jnp.bfloat16)
        hidden_two = jax.nn.silu(jnp.einsum('bhc,bhg->bgc', hidden_one.astype(jnp.float32), middle_w)).astype(jnp.bfloat16)
        return jnp.einsum('bgc,blg->blc', hidden_two.astype(jnp.float32), last_w).astype(jnp.bfloat16)
    outputs = lax.map(apply_group, (grouped, experts))
    flat_out = jnp.transpose(outputs, (2, 0, 1, 3)).reshape(levels, block_total, CMAX)
    cloudy_mask = jnp.arange(CMAX, dtype=jnp.int32)[None, None, :] < cloudy_count[None, :, None]
    masked = jnp.where(cloudy_mask, flat_out, jnp.zeros_like(flat_out))
    padded = jnp.pad(masked, ((0, 0), (0, 0), (0, segment_len - CMAX)))
    return padded.reshape(levels, NLAT, NLON)

def spectral_step(forcing, analysis, table_flat, nudge_rate, band_waves):
    levels = forcing.shape[0]
    spectrum = jnp.fft.rfft(forcing, axis=-1)[..., band_waves] / math.sqrt(NLON)
    fourier = jnp.stack([jnp.real(spectrum), jnp.imag(spectrum)], axis=1)
    spectral = jnp.einsum('lrqs,sqk->lrsk', fourier, table_flat, precision=lax.Precision.HIGHEST) / math.sqrt(NLAT)
    total_wave = (band_waves[:, None] + jnp.arange(K, dtype=jnp.int32)[None, :]).astype(jnp.float32)
    damping = diffusion * total_wave * (total_wave + 1.0) / (M * (M + 1.0))
    rate_view = nudge_rate[:, None, None, None]
    solved = (spectral + time_step * rate_view * analysis) / (1.0 + time_step * (damping[None, None] + rate_view))
    back = jnp.einsum('lrsk,sqk->lrqs', solved, table_flat, precision=lax.Precision.HIGHEST) / math.sqrt(K)
    factor = jnp.where(band_waves == 0, 2.0, 1.0)
    zero_field = jnp.zeros((levels, NLAT, NLON // 2 + 1), jnp.float32)
    full_spectrum = lax.complex(zero_field, zero_field).at[..., band_waves].set(lax.complex(back[:, 0] * factor, back[:, 1] * factor))
    return jnp.fft.irfft(full_spectrum, n=NLON, axis=-1) * (NLON / 2.0) / math.sqrt(M)

def reference(initial_state, prev_tendency, analysis, legendre, nudge_rate, band_waves, cloudy_count, expert_of, w_in, w_mid, w_out):
    tendency = physics(initial_state, cloudy_count, expert_of, w_in, w_mid, w_out)
    table_flat = legendre.reshape(M, NLAT, K)
    current = initial_state
    for step_index in range(STEPS):
        applied = prev_tendency if step_index == 0 else tendency.astype(jnp.float32)
        current = spectral_step(current + time_step * applied, analysis, table_flat, nudge_rate, band_waves)
    return (current, tendency)
```

```python
import math

import jax
import jax.numpy as jnp
import numpy as np
from jax import lax
from jax.sharding import PartitionSpec as P

NB_ROW = 16
CMAX = 128
TIME_STEP = 0.5
HIGH = lax.Precision.HIGH
BOTH = ("dyn", "phys")


def wave_table(waves, n_lon):
    phases = np.arange(waves)[:, None] * np.arange(n_lon)[None, :] % n_lon
    angles = phases.astype(np.float64) * (2.0 * math.pi / n_lon)
    return np.stack([np.cos(angles), -np.sin(angles)], axis=0).astype(np.float32)


def routing(expert_of, n_phys, capacity):
    experts = expert_of[:, 0]
    blocks = experts.shape[0]
    block_order = jnp.arange(blocks, dtype=jnp.int32)
    earlier = (experts[:, None] == experts[None, :]) & (block_order[None, :] < block_order[:, None])
    rank_within = jnp.sum(earlier.astype(jnp.int32), axis=1)
    target = experts * capacity + rank_within
    slots = jnp.arange(n_phys * capacity, dtype=jnp.int32)
    return (target[:, None] == slots[None, :]).astype(jnp.bfloat16)


def physics_local(initial_state, cloudy_count, expert_of, w_in, w_mid, w_out):
    levels, lat_rows, n_lon = initial_state.shape
    n_phys = lax.axis_size("phys")
    blocks = expert_of.shape[0]
    capacity = 2
    columns = initial_state.reshape(levels, blocks, n_lon // NB_ROW).astype(jnp.bfloat16)
    placing = routing(expert_of, n_phys, capacity)
    outgoing = jnp.einsum("bd,lbc->dlc", placing, columns, preferred_element_type=jnp.float32)
    outgoing = outgoing.astype(jnp.bfloat16).reshape(n_phys, capacity, levels, CMAX)
    arrived = lax.all_to_all(outgoing, "phys", split_axis=0, concat_axis=0, tiled=True)
    hidden_one = jax.nn.silu(
        jnp.einsum("qilc,lh->qihc", arrived, w_in[0], preferred_element_type=jnp.float32)
    ).astype(jnp.bfloat16)
    hidden_two = jax.nn.silu(
        jnp.einsum("qihc,hg->qigc", hidden_one, w_mid[0], preferred_element_type=jnp.float32)
    ).astype(jnp.bfloat16)
    computed = jnp.einsum(
        "qigc,lg->qilc", hidden_two, w_out[0], preferred_element_type=jnp.float32
    ).astype(jnp.bfloat16)
    returned = lax.all_to_all(computed, "phys", split_axis=0, concat_axis=0, tiled=True).reshape(
        n_phys * capacity, levels, CMAX
    )
    gathered = jnp.einsum("bd,dlc->lbc", placing, returned, preferred_element_type=jnp.float32)
    cloudy_mask = jnp.arange(CMAX, dtype=jnp.int32)[None, None, :] < cloudy_count[None, :, None]
    masked = jnp.where(cloudy_mask, gathered, 0.0).astype(jnp.bfloat16)
    return masked.reshape(levels, lat_rows, n_lon)


def on_device(
    initial_state,
    prev_tendency,
    analysis,
    legendre,
    nudge_rate,
    band_waves,
    cloudy_count,
    expert_of,
    w_in,
    w_mid,
    w_out,
):
    levels, _, n_lon = initial_state.shape
    waves = band_waves.shape[0]
    coeffs = legendre.shape[3]
    lats = waves
    table = jnp.asarray(wave_table(waves, n_lon))
    wave_ids = jnp.arange(waves, dtype=jnp.int32)
    slot_of = (band_waves[:, None] == wave_ids[None, :]).astype(jnp.bfloat16)
    me = lax.axis_index("dyn") * lax.axis_size("phys") + lax.axis_index("phys")
    own_wave = lax.dynamic_index_in_dim(band_waves, me, 0, keepdims=False)

    def to_slots(field):
        natural = jnp.einsum("lx,rmx->rml", field, table, precision=HIGH) * (1.0 / math.sqrt(n_lon))
        return jnp.einsum(
            "sm,rml->srl", slot_of, natural.astype(jnp.bfloat16), preferred_element_type=jnp.float32
        ).astype(jnp.bfloat16)

    tendency = physics_local(initial_state, cloudy_count, expert_of, w_in, w_mid, w_out)
    first = to_slots(initial_state[:, 0] + TIME_STEP * prev_tendency[:, 0])
    second = to_slots(TIME_STEP * tendency[:, 0].astype(jnp.float32))
    sent = jnp.concatenate([first, second], axis=1)
    got = lax.all_to_all(sent, BOTH, split_axis=0, concat_axis=0, tiled=True)
    got = got.reshape(lats, 2, 2, levels).astype(jnp.float32)

    own_table = lax.all_to_all(
        legendre.astype(jnp.bfloat16), "phys", split_axis=0, concat_axis=2, tiled=True
    ).reshape(lats, coeffs).astype(jnp.float32)

    total_wave = (own_wave + jnp.arange(coeffs, dtype=jnp.int32)).astype(jnp.float32)
    damping = total_wave * (total_wave + 1.0) / (waves * (waves + 1.0))
    rate = nudge_rate[:, None]
    inverse = 1.0 / (1.0 + TIME_STEP * (damping[None, :] + rate))
    pulled = TIME_STEP * rate[None] * analysis[:, :, 0].transpose(1, 0, 2)

    def step(fourier):
        spectral = jnp.einsum("qrl,qk->rlk", fourier, own_table, precision=HIGH) * (
            1.0 / math.sqrt(lats)
        )
        solved = (spectral + pulled) * inverse[None]
        return jnp.einsum("rlk,qk->qrl", solved, own_table, precision=HIGH) * (
            1.0 / math.sqrt(coeffs)
        )

    again = (n_lon / 2.0) / math.sqrt(waves) / math.sqrt(n_lon)
    zero_wave = own_wave == 0
    regain = jnp.stack([jnp.where(zero_wave, 2.0 * again, again), jnp.where(zero_wave, 0.0, again)])
    back = step(got[:, 0])
    back = step(regain[None, :, None] * back + got[:, 1])
    home = lax.all_to_all(back.astype(jnp.bfloat16), BOTH, split_axis=0, concat_axis=0, tiled=True)
    natural = jnp.einsum("sm,srl->rml", slot_of, home, preferred_element_type=jnp.float32)
    final = jnp.einsum("rml,rmx->lx", natural, table, precision=HIGH) * (1.0 / math.sqrt(waves))
    return (final[:, None, :], tendency)


def solution(mesh):
    in_specs = (
        P(None, ("dyn", "phys"), None),
        P(None, ("dyn", "phys"), None),
        P(None, None, ("dyn", "phys"), None),
        P("dyn", None, "phys", None),
        P(),
        P(),
        P(("dyn", "phys")),
        P(("dyn", "phys"), None),
        P("phys", None, None),
        P("phys", None, None),
        P("phys", None, None),
    )
    out_specs = (P(None, ("dyn", "phys"), None), P(None, ("dyn", "phys"), None))
    return jax.shard_map(
        on_device, mesh=mesh, in_specs=in_specs, out_specs=out_specs, check_vma=False
    )
```

```python
import functools
import math

import jax
import jax.numpy as jnp
import numpy as np
from jax import lax
from jax.experimental import pallas as pl
from jax.experimental.pallas import tpu as pltpu
from jax.sharding import PartitionSpec as P

NB_ROW = 16
CMAX = 128
CAP = 2
LANES = 128
TIME_STEP = 0.5
BOTH = ("dyn", "phys")
VMEM = pl.BlockSpec(memory_space=pltpu.VMEM)
SMEM = pl.BlockSpec(memory_space=pltpu.SMEM)
BF16 = jnp.bfloat16
F32 = jnp.float32


def params():
    return pltpu.CompilerParams(vmem_limit_bytes=48 << 20)


def wave_table(waves, n_lon):
    phases = np.arange(waves)[:, None] * np.arange(n_lon)[None, :] % n_lon
    angles = phases.astype(np.float64) * (2.0 * math.pi / n_lon)
    table = np.concatenate([np.cos(angles), -np.sin(angles)], axis=0).astype(np.float32)
    high = table.astype(jnp.bfloat16)
    low = (table - high.astype(np.float32)).astype(jnp.bfloat16)
    return high, low


def dot(a, b):
    return jnp.dot(a, b, preferred_element_type=F32)


def dot_nt(a, b):
    return lax.dot_general(a, b, (((1,), (1,)), ((), ())), preferred_element_type=F32)


def dot_tn(a, b):
    return lax.dot_general(a, b, (((0,), (0,)), ((), ())), preferred_element_type=F32)


def split(value):
    high = value.astype(BF16)
    return high, (value - high.astype(F32)).astype(BF16)


def place_kernel(expert_ref, state_ref, legendre_ref, out_ref, count_ref):
    networks, _, width = out_ref.shape
    blocks = state_ref.shape[1]
    share = legendre_ref.shape[1] // CAP
    out_ref[:, share:, :] = jnp.zeros((networks, out_ref.shape[1] - share, width), BF16)
    for network in range(networks):
        count_ref[network] = 0
        for half in range(CAP):
            part = legendre_ref[network, pl.ds(half, share, stride=CAP), :]
            out_ref[network, :share, half * CMAX : (half + 1) * CMAX] = part.astype(BF16)
    for block in range(blocks):
        network = expert_ref[block]
        rank = count_ref[network]
        count_ref[network] = rank + 1
        lanes = pl.ds(pl.multiple_of(rank * CMAX, CMAX), CMAX)
        out_ref[network, share:, lanes] = state_ref[:, block, :].astype(BF16)


def place_blocks(experts, state, legendre):
    levels = state.shape[0]
    networks, share, _ = legendre.shape
    return pl.pallas_call(
        place_kernel,
        in_specs=[SMEM, VMEM, VMEM],
        out_specs=VMEM,
        out_shape=jax.ShapeDtypeStruct((networks, share // CAP + levels, CAP * CMAX), BF16),
        scratch_shapes=[pltpu.SMEM((networks,), jnp.int32)],
        compiler_params=params(),
        name="place",
    )(experts, state, legendre)


def first_kernel(n_lon, state_ref, prev_ref, order_ref, high_ref, low_ref, table_ref, out_ref):
    levels, blocks, _ = state_ref.shape
    waves = order_ref.shape[0]
    parts = [
        state_ref[:, block, :] + TIME_STEP * prev_ref[:, block, :] for block in range(blocks)
    ]
    forcing = jnp.concatenate(parts, axis=1)
    blank = jnp.zeros((LANES - levels, n_lon), F32)
    high, low = split(jnp.concatenate([forcing, blank], axis=0))
    both = dot_nt(high_ref[...], jnp.concatenate([high, low], axis=0))
    natural = both[:, :LANES] + (both[:, LANES:] + dot_nt(low_ref[...], high))
    natural = (natural * (1.0 / math.sqrt(n_lon))).astype(BF16)
    for part in range(2):
        rows = slice(part * waves, (part + 1) * waves)
        table_ref[rows, :] = dot(order_ref[...], high_ref[rows, :]).astype(BF16)
        out_ref[rows, :] = dot(order_ref[...], natural[rows, :]).astype(BF16)


def first_transform(state, prev, order, high, low):
    rows, n_lon = high.shape
    return pl.pallas_call(
        functools.partial(first_kernel, n_lon),
        in_specs=[VMEM] * 5,
        out_specs=[VMEM] * 2,
        out_shape=[
            jax.ShapeDtypeStruct((rows, n_lon), BF16),
            jax.ShapeDtypeStruct((rows, LANES), BF16),
        ],
        compiler_params=params(),
        cost_estimate=pl.CostEstimate(
            flops=4 * rows * n_lon * rows, bytes_accessed=8 << 20, transcendentals=0
        ),
        name="first",
    )(state, prev, order, high, low)


def half_silu(half):
    return (half + half * jnp.tanh(half)).astype(BF16)


def network_kernel(skip, group, x_ref, first_ref, middle_ref, last_ref, out_ref):
    width = x_ref.shape[2]
    for start in range(0, x_ref.shape[0], group):
        columns = jnp.concatenate([x_ref[start + i, skip:, :] for i in range(group)], axis=1)
        one = half_silu(dot(first_ref[...], columns))
        two = half_silu(dot(middle_ref[...], one))
        out = dot(last_ref[...], two).astype(BF16)
        for i in range(group):
            out_ref[start + i] = out[:, i * width : (i + 1) * width]


def network(arrived, first_w, middle_w, last_w):
    senders, rows, width = arrived.shape
    levels, hidden = last_w.shape
    step = 4
    return pl.pallas_call(
        functools.partial(network_kernel, rows - levels, 2),
        grid=(senders // step,),
        in_specs=[
            pl.BlockSpec((step, rows, width), lambda i: (i, 0, 0)),
            pl.BlockSpec((hidden, levels), lambda i: (0, 0)),
            pl.BlockSpec((hidden, hidden), lambda i: (0, 0)),
            pl.BlockSpec((levels, hidden), lambda i: (0, 0)),
        ],
        out_specs=pl.BlockSpec((step, levels, width), lambda i: (i, 0, 0)),
        out_shape=jax.ShapeDtypeStruct((senders, levels, width), BF16),
        compiler_params=params(),
        cost_estimate=pl.CostEstimate(
            flops=2 * senders * width * hidden * (hidden + 2 * 256),
            bytes_accessed=4 << 20,
            transcendentals=2 * senders * width * hidden,
        ),
        name="network",
    )(arrived, first_w, middle_w, last_w)


def return_kernel(
    n_lon, expert_ref, cloudy_ref, returned_ref, table_ref, first_ref, tend_ref, out_ref, count_ref, rows_ref
):
    networks, levels, _ = returned_ref.shape
    waves = first_ref.shape[0] // 2
    lanes = lax.broadcasted_iota(jnp.int32, (levels, CMAX), 1)
    for network in range(networks):
        count_ref[network] = 0
    for block in range(NB_ROW):
        network = expert_ref[block]
        rank = count_ref[network]
        count_ref[network] = rank + 1
        place = pl.ds(pl.multiple_of(rank * CMAX, CMAX), CMAX)
        values = returned_ref[network, :, place].astype(F32)
        kept = jnp.where(lanes < cloudy_ref[block], values, 0.0)
        tend_ref[:, block * CMAX : (block + 1) * CMAX] = kept.astype(BF16)
    out = dot_nt(table_ref[...], tend_ref[...]) * (TIME_STEP / math.sqrt(n_lon))
    out = jnp.concatenate([out, jnp.zeros((out.shape[0], LANES - levels), F32)], axis=1)
    for part in range(2):
        rows = slice(part * waves, (part + 1) * waves)
        rows_ref[pl.ds(part, waves, stride=4), :] = first_ref[rows, :].astype(F32)
        rows_ref[pl.ds(2 + part, waves, stride=4), :] = out[rows]
    out_ref[...] = rows_ref[...].astype(BF16)


def return_blocks(experts, cloudy, returned, table, first):
    rows, n_lon = table.shape
    networks, levels, _ = returned.shape
    return pl.pallas_call(
        functools.partial(return_kernel, n_lon),
        in_specs=[SMEM, SMEM, VMEM, VMEM, VMEM],
        out_specs=[VMEM] * 2,
        out_shape=[
            jax.ShapeDtypeStruct((levels, n_lon), BF16),
            jax.ShapeDtypeStruct((2 * rows, LANES), BF16),
        ],
        scratch_shapes=[pltpu.SMEM((networks,), jnp.int32), pltpu.VMEM((2 * rows, LANES), F32)],
        compiler_params=params(),
        name="return",
    )(experts, cloudy, returned, table, first)


def solve_kernel(got_ref, there_ref, back_ref, gain_ref, pull_ref, regain_ref, out_ref, rows_ref, turn_ref):
    lats = back_ref.shape[0]
    rows_ref[...] = got_ref[...].astype(F32)
    parts = [rows_ref[pl.ds(part, lats, stride=4), :].astype(BF16) for part in range(4)]

    def twice(table_ref, value):
        both = dot(table_ref[...], jnp.concatenate(split(value), axis=1))
        return both[:, : 2 * LANES] + both[:, 2 * LANES :]

    spectral = dot(there_ref[...], jnp.concatenate(parts, axis=1))
    gain = gain_ref[...]
    pull = pull_ref[...]
    back = twice(back_ref, spectral[:, : 2 * LANES] * gain + pull)
    again = spectral[:, 2 * LANES :] + twice(there_ref, back * regain_ref[...])
    final = twice(back_ref, again * gain + pull)
    for part in range(2):
        turn_ref[pl.ds(part, lats, stride=2), :] = final[:, part * LANES : (part + 1) * LANES]
    out_ref[...] = turn_ref[...].astype(BF16)


def solve_twice(got, there, back, gain, pull, regain):
    rows = got.shape[0]
    return pl.pallas_call(
        solve_kernel,
        in_specs=[VMEM] * 6,
        out_specs=VMEM,
        out_shape=jax.ShapeDtypeStruct((rows // 2, LANES), BF16),
        scratch_shapes=[pltpu.VMEM((rows, LANES), F32), pltpu.VMEM((rows // 2, LANES), F32)],
        compiler_params=params(),
        name="solve",
    )(got, there, back, gain, pull, regain)


def synthesis_kernel(scale, home_ref, table_ref, out_ref, rows_ref):
    levels, blocks, width = out_ref.shape
    waves = home_ref.shape[0] // 2
    rows_ref[...] = home_ref[...].astype(F32)
    parts = [rows_ref[pl.ds(part, waves, stride=2), :].astype(BF16) for part in range(2)]
    grid = dot_tn(jnp.concatenate(parts, axis=0), table_ref[...]) * scale
    for block in range(blocks):
        out_ref[:, block, :] = grid[:levels, block * width : (block + 1) * width]


def synthesis(home, table, levels, scale):
    n_lon = table.shape[1]
    return pl.pallas_call(
        functools.partial(synthesis_kernel, scale),
        in_specs=[VMEM] * 2,
        out_specs=VMEM,
        out_shape=jax.ShapeDtypeStruct((levels, NB_ROW, n_lon // NB_ROW), F32),
        scratch_shapes=[pltpu.VMEM(home.shape, F32)],
        compiler_params=params(),
        name="synthesis",
    )(home, table)


def on_device(
    initial_state,
    prev_tendency,
    analysis,
    legendre,
    nudge_rate,
    band_waves,
    cloudy_count,
    expert_of,
    w_in,
    w_mid,
    w_out,
):
    levels, _, n_lon = initial_state.shape
    n_phys = lax.axis_size("phys")
    waves = band_waves.shape[0]
    coeffs = legendre.shape[3]
    lats = waves
    rows = 2 * waves
    state = initial_state.reshape(levels, NB_ROW, n_lon // NB_ROW)
    prev = prev_tendency.reshape(levels, NB_ROW, n_lon // NB_ROW)
    experts = expert_of[:, 0]

    share = lats // n_phys

    outgoing = place_blocks(experts, state, legendre.reshape(n_phys, share * CAP, coeffs // CAP))
    arrived = lax.all_to_all(outgoing, "phys", split_axis=0, concat_axis=0, tiled=True)
    first_w = (w_in[0] * 0.5).T
    middle_w = (w_mid[0] * 0.5).T
    computed = network(arrived, first_w, middle_w, w_out[0])
    returned = lax.all_to_all(computed, "phys", split_axis=0, concat_axis=0, tiled=True)

    state, prev, analysis, band_waves, computed = lax.optimization_barrier(
        (state, prev, analysis, band_waves, computed)
    )
    high, low = (jnp.asarray(part) for part in wave_table(waves, n_lon))
    order = (band_waves[:, None] == jnp.arange(waves, dtype=jnp.int32)[None, :]).astype(BF16)
    table, first = first_transform(state, prev, order, high, low)
    back_table = arrived[:, :share, :].transpose(1, 0, 2).reshape(lats, coeffs)
    there_table = back_table.T
    me = lax.axis_index("dyn") * n_phys + lax.axis_index("phys")
    own_wave = lax.dynamic_index_in_dim(band_waves, me, 0, keepdims=False)
    total_wave = (own_wave + jnp.arange(coeffs, dtype=jnp.int32)).astype(F32)
    damping = total_wave * (total_wave + 1.0) / (waves * (waves + 1.0))
    rate = jnp.pad(nudge_rate, (0, LANES - levels))
    rate = jnp.concatenate([rate, rate])[None, :]
    inverse = 1.0 / (1.0 + TIME_STEP * (damping[:, None] + rate))
    pulled = jnp.pad(analysis[:, :, 0].transpose(2, 1, 0), ((0, 0), (0, 0), (0, LANES - levels)))
    pulled = pulled.reshape(coeffs, 2 * LANES) * (TIME_STEP * rate) * inverse
    gain = inverse * (1.0 / math.sqrt(lats) / math.sqrt(coeffs))
    pull = pulled * (1.0 / math.sqrt(coeffs))
    again = (n_lon / 2.0) / math.sqrt(waves) / math.sqrt(n_lon)
    zero_wave = own_wave == 0
    regain = jnp.stack([jnp.where(zero_wave, 2.0 * again, again), jnp.where(zero_wave, 0.0, again)])
    regain = jnp.repeat(regain, LANES)[None, :]

    tendency, sent = return_blocks(experts, cloudy_count, returned, table, first)
    got = lax.all_to_all(
        sent.reshape(waves, 4, LANES), BOTH, split_axis=0, concat_axis=0, tiled=True
    )
    back = solve_twice(got.reshape(4 * lats, LANES), there_table, back_table, gain, pull, regain)
    home = lax.all_to_all(
        back.reshape(lats, 2, LANES), BOTH, split_axis=0, concat_axis=0, tiled=True
    )
    final = synthesis(home.reshape(rows, LANES), table, levels, 1.0 / math.sqrt(waves))
    return (final.reshape(levels, 1, n_lon), tendency.reshape(levels, 1, n_lon))


def solution(mesh):
    in_specs = (
        P(None, ("dyn", "phys"), None),
        P(None, ("dyn", "phys"), None),
        P(None, None, ("dyn", "phys"), None),
        P("dyn", None, "phys", None),
        P(),
        P(),
        P(("dyn", "phys")),
        P(("dyn", "phys"), None),
        P("phys", None, None),
        P("phys", None, None),
        P("phys", None, None),
    )
    out_specs = (P(None, ("dyn", "phys"), None), P(None, ("dyn", "phys"), None))
    return jax.shard_map(
        on_device, mesh=mesh, in_specs=in_specs, out_specs=out_specs, check_vma=False
    )
```

```python
import functools
import math

import jax
import jax.numpy as jnp
import numpy as np
from jax import lax
from jax.experimental import pallas as pl
from jax.experimental.pallas import tpu as pltpu
from jax.sharding import PartitionSpec as P

NB_ROW = 16
CMAX = 128
CAP = 2
LANES = 128
TIME_STEP = 0.5
ORDER = ("phys", "dyn")
VMEM = pl.BlockSpec(memory_space=pltpu.VMEM)
SMEM = pl.BlockSpec(memory_space=pltpu.SMEM)
HBM = pl.BlockSpec(memory_space=pltpu.HBM)
BF16 = jnp.bfloat16
F32 = jnp.float32


def params(mebibytes=32):
    return pltpu.CompilerParams(vmem_limit_bytes=mebibytes << 20)


def in_hbm(*arrays):
    return [pltpu.with_memory_space_constraint(array, pltpu.HBM) for array in arrays]


def wave_table(waves, n_lon):
    phases = np.arange(waves)[:, None] * np.arange(n_lon)[None, :] % n_lon
    angles = phases.astype(np.float64) * (2.0 * math.pi / n_lon)
    table = np.concatenate([np.cos(angles), -np.sin(angles)], axis=0).astype(np.float32)
    high = table.astype(jnp.bfloat16)
    low = (table - high.astype(np.float32)).astype(jnp.bfloat16)
    return high, low


def dot(a, b):
    return jnp.dot(a, b, preferred_element_type=F32)


def dot_nt(a, b):
    return lax.dot_general(a, b, (((1,), (1,)), ((), ())), preferred_element_type=F32)


def dot_tn(a, b):
    return lax.dot_general(a, b, (((0,), (0,)), ((), ())), preferred_element_type=F32)


def split(value):
    high = value.astype(BF16)
    return high, (value - high.astype(F32)).astype(BF16)


def place_kernel(
    expert_hbm, state_hbm, legendre_hbm, out_ref, expert_ref, state_ref, legendre_ref, count_ref, sems
):
    networks, _, width = out_ref.shape
    blocks, levels, _ = state_ref.shape
    share = legendre_ref.shape[1] // CAP
    fetches = [
        pltpu.make_async_copy(state_hbm.at[:, block, :], state_ref.at[block], sems.at[block])
        for block in range(blocks)
    ]
    expert_fetch = pltpu.make_async_copy(expert_hbm, expert_ref, sems.at[blocks])
    legendre_fetch = pltpu.make_async_copy(legendre_hbm, legendre_ref, sems.at[blocks + 1])
    expert_fetch.start()
    legendre_fetch.start()
    for fetch in fetches:
        fetch.start()
    out_ref[:, share:, :] = jnp.zeros((networks, levels, width), BF16)
    for network in range(networks):
        count_ref[network] = 0
    expert_fetch.wait()
    legendre_fetch.wait()
    for network in range(networks):
        for half in range(CAP):
            part = legendre_ref[network, pl.ds(half, share, stride=CAP), :]
            out_ref[network, :share, half * CMAX : (half + 1) * CMAX] = part.astype(BF16)
    for block in range(blocks):
        network = expert_ref[block]
        rank = count_ref[network]
        count_ref[network] = rank + 1
        lanes = pl.ds(pl.multiple_of(rank * CMAX, CMAX), CMAX)
        fetches[block].wait()
        out_ref[network, share:, lanes] = (0.5 * state_ref[block]).astype(BF16)


def place_blocks(experts, state, legendre):
    levels, blocks, width = state.shape
    networks, share, _ = legendre.shape
    return pl.pallas_call(
        place_kernel,
        in_specs=[HBM] * 3,
        out_specs=VMEM,
        out_shape=pltpu.HBM((networks, share // CAP + levels, CAP * CMAX), BF16),
        scratch_shapes=[
            pltpu.SMEM((blocks,), jnp.int32),
            pltpu.VMEM((blocks, levels, width), F32),
            pltpu.VMEM(legendre.shape, F32),
            pltpu.SMEM((networks,), jnp.int32),
            pltpu.SemaphoreType.DMA((blocks + 2,)),
        ],
        compiler_params=params(),
        name="place",
    )(*in_hbm(experts, state, legendre))


def prepare_kernel(
    n_lon, order_ref, state_hbm, prev_hbm, high_hbm, low_hbm, in_hbm, mid_hbm, last_hbm,
    table_ref, out_ref, first_ref, middle_ref, last_ref,
    state_ref, prev_ref, high_ref, low_ref, in_ref, mid_ref, sems
):
    levels, blocks, _ = state_ref.shape
    waves = order_ref.shape[0]
    pairs = (
        (mid_hbm, mid_ref), (in_hbm, in_ref), (last_hbm, last_ref),
        (high_hbm, high_ref), (state_hbm, state_ref), (prev_hbm, prev_ref), (low_hbm, low_ref),
    )
    fetches = [
        pltpu.make_async_copy(source, target, sems.at[i]) for i, (source, target) in enumerate(pairs)
    ]
    for fetch in fetches:
        fetch.start()
    for fetch in fetches[:4]:
        fetch.wait()
    side = waves
    diagonal = lax.broadcasted_iota(jnp.int32, (side, side), 0) == lax.broadcasted_iota(
        jnp.int32, (side, side), 1
    )
    half = jnp.where(diagonal, 0.5, 0.0).astype(BF16)
    for start in range(0, mid_ref.shape[1], side):
        rows = slice(start, start + side)
        middle_ref[rows, :] = dot_nt(half, mid_ref[:, rows]).astype(BF16)
        first_ref[rows, :] = (2.0 * dot_nt(half, in_ref[:, rows])).astype(BF16)
    for part in range(2):
        rows = slice(part * waves, (part + 1) * waves)
        table_ref[rows, :] = dot(order_ref[...], high_ref[rows, :]).astype(BF16)
    for fetch in fetches[4:]:
        fetch.wait()
    parts = [
        state_ref[:, block, :] + TIME_STEP * prev_ref[:, block, :] for block in range(blocks)
    ]
    forcing = jnp.concatenate(parts, axis=1)
    blank = jnp.zeros((LANES - levels, n_lon), F32)
    high, low = split(jnp.concatenate([forcing, blank], axis=0))
    both = dot_nt(high_ref[...], jnp.concatenate([high, low], axis=0))
    natural = both[:, :LANES] + (both[:, LANES:] + dot_nt(low_ref[...], high))
    natural = (natural * (1.0 / math.sqrt(n_lon))).astype(BF16)
    for part in range(2):
        rows = slice(part * waves, (part + 1) * waves)
        out_ref[rows, :] = dot(order_ref[...], natural[rows, :]).astype(BF16)


def prepare(state, prev, order, high, low, w_in, w_mid, w_out):
    rows, n_lon = high.shape
    levels, hidden = w_in.shape
    return pl.pallas_call(
        functools.partial(prepare_kernel, n_lon),
        in_specs=[VMEM] + [HBM] * 7,
        out_specs=[VMEM] * 5,
        out_shape=[
            pltpu.HBM((rows, n_lon), BF16),
            pltpu.HBM((rows, LANES), BF16),
            jax.ShapeDtypeStruct((hidden, levels), BF16),
            jax.ShapeDtypeStruct((hidden, hidden), BF16),
            jax.ShapeDtypeStruct((levels, hidden), BF16),
        ],
        scratch_shapes=[
            pltpu.VMEM(state.shape, F32),
            pltpu.VMEM(prev.shape, F32),
            pltpu.VMEM(high.shape, BF16),
            pltpu.VMEM(low.shape, BF16),
            pltpu.VMEM(w_in.shape, BF16),
            pltpu.VMEM(w_mid.shape, BF16),
            pltpu.SemaphoreType.DMA((7,)),
        ],
        compiler_params=params(),
        cost_estimate=pl.CostEstimate(
            flops=4 * rows * n_lon * rows, bytes_accessed=12 << 20, transcendentals=0
        ),
        name="prepare",
    )(order, *in_hbm(state, prev, high, low, w_in, w_mid, w_out))


def silu(half):
    return (half + half * jnp.tanh(half)).astype(BF16)


def network_kernel(skip, group, x_ref, first_ref, middle_ref, last_ref, out_ref, own_ref):
    width = x_ref.shape[2]
    own_ref[...] = x_ref[:, :skip, :]
    for start in range(0, x_ref.shape[0], group):
        columns = jnp.concatenate([x_ref[start + i, skip:, :] for i in range(group)], axis=1)
        one = silu(dot(first_ref[...], columns))
        two = silu(dot(middle_ref[...], one))
        out = dot(last_ref[...], two).astype(BF16)
        for i in range(group):
            out_ref[start + i] = out[:, i * width : (i + 1) * width]


def network(arrived, first_w, middle_w, last_w):
    senders, rows, width = arrived.shape
    levels, hidden = last_w.shape
    step = 4
    return pl.pallas_call(
        functools.partial(network_kernel, rows - levels, 2),
        grid=(senders // step,),
        in_specs=[
            pl.BlockSpec((step, rows, width), lambda i: (i, 0, 0)),
            pl.BlockSpec((hidden, levels), lambda i: (0, 0)),
            pl.BlockSpec((hidden, hidden), lambda i: (0, 0)),
            pl.BlockSpec((levels, hidden), lambda i: (0, 0)),
        ],
        out_specs=[
            pl.BlockSpec((step, levels, width), lambda i: (i, 0, 0)),
            pl.BlockSpec((step, rows - levels, width), lambda i: (i, 0, 0)),
        ],
        out_shape=[
            jax.ShapeDtypeStruct((senders, levels, width), BF16),
            pltpu.HBM((senders, rows - levels, width), BF16),
        ],
        compiler_params=params(),
        cost_estimate=pl.CostEstimate(
            flops=2 * senders * width * hidden * (hidden + 2 * 256),
            bytes_accessed=4 << 20,
            transcendentals=2 * senders * width * hidden,
        ),
        name="network",
    )(arrived, first_w, middle_w, last_w)


def return_kernel(
    n_lon, returned_ref, expert_hbm, cloudy_hbm, table_hbm, first_hbm, tend_ref, out_ref,
    expert_ref, cloudy_ref, table_ref, first_ref, count_ref, rows_ref, sems
):
    networks, levels, _ = returned_ref.shape
    waves = first_ref.shape[0] // 2
    pairs = (
        (expert_hbm, expert_ref), (cloudy_hbm, cloudy_ref), (table_hbm, table_ref), (first_hbm, first_ref),
    )
    fetches = [
        pltpu.make_async_copy(source, target, sems.at[i]) for i, (source, target) in enumerate(pairs)
    ]
    for fetch in fetches:
        fetch.start()
    lanes = lax.broadcasted_iota(jnp.int32, (levels, CMAX), 1)
    for network in range(networks):
        count_ref[network] = 0
    for fetch in fetches[:2]:
        fetch.wait()
    for block in range(NB_ROW):
        network = expert_ref[block]
        rank = count_ref[network]
        count_ref[network] = rank + 1
        place = pl.ds(pl.multiple_of(rank * CMAX, CMAX), CMAX)
        values = returned_ref[network, :, place].astype(F32)
        kept = jnp.where(lanes < cloudy_ref[block], values, 0.0)
        tend_ref[:, block * CMAX : (block + 1) * CMAX] = kept.astype(BF16)
    for fetch in fetches[2:]:
        fetch.wait()
    out = dot_nt(table_ref[...], tend_ref[...]) * (TIME_STEP / math.sqrt(n_lon))
    out = jnp.concatenate([out, jnp.zeros((out.shape[0], LANES - levels), F32)], axis=1)
    for part in range(2):
        rows = slice(part * waves, (part + 1) * waves)
        rows_ref[pl.ds(part, waves, stride=4), :] = first_ref[rows, :].astype(F32)
        rows_ref[pl.ds(2 + part, waves, stride=4), :] = out[rows]
    out_ref[...] = rows_ref[...].astype(BF16)


def return_blocks(returned, experts, cloudy, table, first):
    rows, n_lon = table.shape
    networks, levels, _ = returned.shape
    return pl.pallas_call(
        functools.partial(return_kernel, n_lon),
        in_specs=[VMEM] + [HBM] * 4,
        out_specs=[VMEM] * 2,
        out_shape=[
            pltpu.HBM((levels, n_lon), BF16),
            jax.ShapeDtypeStruct((2 * rows, LANES), BF16),
        ],
        scratch_shapes=[
            pltpu.SMEM(experts.shape, jnp.int32),
            pltpu.SMEM(cloudy.shape, jnp.int32),
            pltpu.VMEM(table.shape, BF16),
            pltpu.VMEM(first.shape, BF16),
            pltpu.SMEM((networks,), jnp.int32),
            pltpu.VMEM((2 * rows, LANES), F32),
            pltpu.SemaphoreType.DMA((4,)),
        ],
        compiler_params=params(),
        name="return",
    )(returned, *in_hbm(experts, cloudy, table, first))


def solve_kernel(
    scale, again, me_ref, got_ref, wave_hbm, own_hbm, analysis_hbm, rate_hbm, out_ref,
    wave_ref, own_ref, analysis_ref, rate_ref, rows_ref, turn_ref, sems
):
    levels = analysis_ref.shape[0]
    networks, share, coeffs = own_ref.shape
    lats = networks * share
    pairs = (
        (wave_hbm, wave_ref), (own_hbm, own_ref), (analysis_hbm, analysis_ref), (rate_hbm, rate_ref),
    )
    fetches = [
        pltpu.make_async_copy(source, target, sems.at[i]) for i, (source, target) in enumerate(pairs)
    ]
    for fetch in fetches:
        fetch.start()
    rows_ref[...] = got_ref[...].astype(F32)
    parts = [rows_ref[pl.ds(part, lats, stride=4), :].astype(BF16) for part in range(4)]
    for fetch in fetches:
        fetch.wait()
    table = jnp.concatenate([own_ref[sender] for sender in range(networks)], axis=0)

    wave = wave_ref[me_ref[0]]
    total = (wave + lax.broadcasted_iota(jnp.int32, (levels, coeffs), 1)).astype(F32)
    rate = jnp.concatenate([rate_ref[...], jnp.zeros((1, LANES - levels), F32)], axis=1)
    rate = jnp.broadcast_to(rate, (LANES, LANES)).T[:levels]
    rate = jnp.concatenate([rate, rate], axis=1)
    inverse = 1.0 / (1.0 + TIME_STEP * (total * (total + 1.0) * scale + rate))
    blank = jnp.zeros((LANES - levels, coeffs), F32)
    gains, pulls = [], []
    for part in range(2):
        halves = [analysis_ref[:, 2 * part + half, :] for half in range(2)]
        pulled = TIME_STEP * rate * jnp.concatenate(halves, axis=1) * inverse
        gains += [inverse * (1.0 / lats), blank]
        pulls += [pulled * (1.0 / math.sqrt(coeffs)), blank]
    gain = jnp.concatenate(gains, axis=0)
    pull = jnp.concatenate(pulls, axis=0)
    real = jnp.where(wave == 0, 2.0 * again, again)
    imag = jnp.where(wave == 0, 0.0, again)
    lane = lax.broadcasted_iota(jnp.int32, (1, 2 * LANES), 1)
    regain = jnp.where(lane < LANES, real, imag)

    def there(value):
        both = dot_tn(jnp.concatenate(split(value), axis=1), table)
        return both[: 2 * LANES] + both[2 * LANES :]

    def back(value):
        both = dot_nt(table, jnp.concatenate(split(value), axis=0))
        return both[:, : 2 * LANES] + both[:, 2 * LANES :]

    spectral = dot_tn(jnp.concatenate(parts, axis=1), table)
    first = back(spectral[: 2 * LANES] * gain + pull)
    second = spectral[2 * LANES :] + there(first * regain)
    final = back(second * gain + pull)
    for part in range(2):
        turn_ref[pl.ds(part, lats, stride=2), :] = final[:, part * LANES : (part + 1) * LANES]
    out_ref[...] = turn_ref[...].astype(BF16)


def solve_twice(scale, again, me, got, waves, own, analysis, rate):
    rows = got.shape[0]
    return pl.pallas_call(
        functools.partial(solve_kernel, scale, again),
        in_specs=[SMEM, VMEM] + [HBM] * 4,
        out_specs=VMEM,
        out_shape=jax.ShapeDtypeStruct((rows // 2, LANES), BF16),
        scratch_shapes=[
            pltpu.SMEM(waves.shape, jnp.int32),
            pltpu.VMEM(own.shape, BF16),
            pltpu.VMEM(analysis.shape, F32),
            pltpu.VMEM(rate.shape, F32),
            pltpu.VMEM((rows, LANES), F32),
            pltpu.VMEM((rows // 2, LANES), F32),
            pltpu.SemaphoreType.DMA((4,)),
        ],
        compiler_params=params(),
        name="solve",
    )(me, got, *in_hbm(waves, own, analysis, rate))


def synthesis_kernel(scale, home_ref, table_ref, out_ref, rows_ref):
    levels, blocks, width = out_ref.shape
    waves = home_ref.shape[0] // 2
    rows_ref[...] = home_ref[...].astype(F32)
    parts = [rows_ref[pl.ds(part, waves, stride=2), :].astype(BF16) for part in range(2)]
    grid = dot_tn(jnp.concatenate(parts, axis=0), table_ref[...]) * scale
    for block in range(blocks):
        out_ref[:, block, :] = grid[:levels, block * width : (block + 1) * width]


def synthesis(home, table, levels, scale):
    n_lon = table.shape[1]
    return pl.pallas_call(
        functools.partial(synthesis_kernel, scale),
        in_specs=[VMEM] * 2,
        out_specs=VMEM,
        out_shape=jax.ShapeDtypeStruct((levels, NB_ROW, n_lon // NB_ROW), F32),
        scratch_shapes=[pltpu.VMEM(home.shape, F32)],
        compiler_params=params(),
        name="synthesis",
    )(home, table)


def on_device(
    initial_state,
    prev_tendency,
    analysis,
    legendre,
    nudge_rate,
    band_waves,
    cloudy_count,
    expert_of,
    w_in,
    w_mid,
    w_out,
):
    levels, _, n_lon = initial_state.shape
    n_dyn = lax.axis_size("dyn")
    n_phys = lax.axis_size("phys")
    waves = band_waves.shape[0]
    coeffs = legendre.shape[3]
    lats = waves
    rows = 2 * waves
    state = initial_state.reshape(levels, NB_ROW, n_lon // NB_ROW)
    prev = prev_tendency.reshape(levels, NB_ROW, n_lon // NB_ROW)
    experts = expert_of[:, 0]

    share = lats // n_phys

    outgoing = place_blocks(experts, state, legendre.reshape(n_phys, share * CAP, coeffs // CAP))
    arrived = lax.all_to_all(outgoing, "phys", split_axis=0, concat_axis=0, tiled=True)

    high, low = (jnp.asarray(part) for part in wave_table(waves, n_lon))
    chunk_waves = band_waves.reshape(n_dyn, n_phys).T.reshape(waves, 1)
    order = (chunk_waves == jnp.arange(waves, dtype=jnp.int32)[None, :]).astype(BF16)
    table, first, first_w, middle_w, last_w = prepare(
        state, prev, order, high, low, w_in[0], w_mid[0], w_out[0]
    )
    me = lax.axis_index("dyn") * n_phys + lax.axis_index("phys")
    arrived, table, first, first_w, middle_w, last_w = lax.optimization_barrier(
        (arrived, table, first, first_w, middle_w, last_w)
    )
    computed, own = network(arrived, first_w, middle_w, last_w)
    returned = lax.all_to_all(computed, "phys", split_axis=0, concat_axis=0, tiled=True)

    tendency, sent = return_blocks(returned, experts, cloudy_count, table, first)
    got = lax.all_to_all(
        sent.reshape(waves, 4, LANES), ORDER, split_axis=0, concat_axis=0, tiled=True
    )
    back = solve_twice(
        1.0 / (waves * (waves + 1.0)),
        (n_lon / 2.0) / math.sqrt(waves) / math.sqrt(n_lon),
        me.reshape(1),
        got.reshape(4 * lats, LANES),
        band_waves,
        own,
        analysis.reshape(levels, 2 * coeffs // LANES, LANES),
        nudge_rate[None, :],
    )
    home = lax.all_to_all(
        back.reshape(lats, 2, LANES), ORDER, split_axis=0, concat_axis=0, tiled=True
    )
    final = synthesis(home.reshape(rows, LANES), table, levels, 1.0 / math.sqrt(waves))
    return (final.reshape(levels, 1, n_lon), tendency.reshape(levels, 1, n_lon))


def solution(mesh):
    in_specs = (
        P(None, ("dyn", "phys"), None),
        P(None, ("dyn", "phys"), None),
        P(None, None, ("dyn", "phys"), None),
        P("dyn", None, "phys", None),
        P(),
        P(),
        P(("dyn", "phys")),
        P(("dyn", "phys"), None),
        P("phys", None, None),
        P("phys", None, None),
        P("phys", None, None),
    )
    out_specs = (P(None, ("dyn", "phys"), None), P(None, ("dyn", "phys"), None))
    return jax.shard_map(
        on_device, mesh=mesh, in_specs=in_specs, out_specs=out_specs, check_vma=False
    )
```

```python
import functools
import math

import jax
import jax.numpy as jnp
import numpy as np
from jax import lax
from jax.experimental import pallas as pl
from jax.experimental.pallas import tpu as pltpu
from jax.sharding import PartitionSpec as P

NB_ROW = 16
CMAX = 128
CAP = 2
LANES = 128
MARK = 1e30
GROUP = 512
TIME_STEP = 0.5
ORDER = ("phys", "dyn")
VMEM = pl.BlockSpec(memory_space=pltpu.VMEM)
SMEM = pl.BlockSpec(memory_space=pltpu.SMEM)
HBM = pl.BlockSpec(memory_space=pltpu.HBM)
BF16 = jnp.bfloat16
F32 = jnp.float32


def params(mebibytes=32):
    return pltpu.CompilerParams(vmem_limit_bytes=mebibytes << 20)


def in_hbm(*arrays):
    return [pltpu.with_memory_space_constraint(array, pltpu.HBM) for array in arrays]


def wave_table(waves, n_lon):
    phases = np.arange(waves)[:, None] * np.arange(n_lon)[None, :] % n_lon
    angles = phases.astype(np.float64) * (2.0 * math.pi / n_lon)
    table = np.concatenate([np.cos(angles), -np.sin(angles)], axis=0).astype(np.float32)
    high = table.astype(jnp.bfloat16)
    low = (table - high.astype(np.float32)).astype(jnp.bfloat16)
    return high, low


def dot(a, b):
    return jnp.dot(a, b, preferred_element_type=F32)


def dot_nt(a, b):
    return lax.dot_general(a, b, (((1,), (1,)), ((), ())), preferred_element_type=F32)


def dot_tn(a, b):
    return lax.dot_general(a, b, (((0,), (0,)), ((), ())), preferred_element_type=F32)


def split(value):
    high = value.astype(BF16)
    return high, (value - high.astype(F32)).astype(BF16)


def place_kernel(
    expert_hbm, cloudy_hbm, state_hbm, legendre_hbm, out_ref,
    expert_ref, cloudy_ref, state_ref, legendre_ref, chunk_ref, used_ref, sems
):
    networks, _, width = out_ref.shape
    blocks, levels, _ = state_ref.shape
    share = legendre_ref.shape[1] // CAP
    fetches = [
        pltpu.make_async_copy(state_hbm.at[:, block, :], state_ref.at[block], sems.at[block])
        for block in range(blocks)
    ]
    pairs = ((expert_hbm, expert_ref), (cloudy_hbm, cloudy_ref), (legendre_hbm, legendre_ref))
    early = [
        pltpu.make_async_copy(source, target, sems.at[blocks + i])
        for i, (source, target) in enumerate(pairs)
    ]
    for fetch in early + fetches:
        fetch.start()
    chunk_ref[...] = jnp.full((networks, levels, width), MARK, F32)
    for network in range(networks):
        used_ref[network] = 0
    for fetch in early:
        fetch.wait()
    for network in range(networks):
        for half in range(CAP):
            part = legendre_ref[network, pl.ds(half, share, stride=CAP), :]
            out_ref[network, :share, half * CMAX : (half + 1) * CMAX] = part.astype(BF16)
    lane = lax.broadcasted_iota(jnp.int32, (levels, CMAX), 1)
    spans = []
    for block in range(blocks):
        network = expert_ref[block]
        start = used_ref[network]
        end = start + cloudy_ref[block]
        used_ref[network] = end
        spans.append((network, start, end))
    for fetch in fetches:
        fetch.wait()
    for block, (network, start, end) in enumerate(spans):
        turned = pltpu.roll(0.5 * state_ref[block], lax.rem(start, CMAX), 1)
        here = (lane >= start) & (lane < end)
        pltpu.store(chunk_ref.at[network, :, :CMAX], turned, mask=here)
        pltpu.store(chunk_ref.at[network, :, CMAX:], turned, mask=lane + CMAX < end)
    out_ref[:, share:, :] = chunk_ref[...].astype(BF16)


def place_blocks(experts, cloudy, state, legendre):
    levels, blocks, width = state.shape
    networks, share, _ = legendre.shape
    return pl.pallas_call(
        place_kernel,
        in_specs=[HBM] * 4,
        out_specs=VMEM,
        out_shape=pltpu.HBM((networks, share // CAP + levels, CAP * CMAX), BF16),
        scratch_shapes=[
            pltpu.SMEM((blocks,), jnp.int32),
            pltpu.SMEM((blocks,), jnp.int32),
            pltpu.VMEM((blocks, levels, width), F32),
            pltpu.VMEM(legendre.shape, F32),
            pltpu.VMEM((networks, levels, CAP * CMAX), F32),
            pltpu.SMEM((networks,), jnp.int32),
            pltpu.SemaphoreType.DMA((blocks + 3,)),
        ],
        compiler_params=params(),
        name="place",
    )(*in_hbm(experts, cloudy, state, legendre))


def prepare_kernel(
    n_lon, order_ref, state_hbm, prev_hbm, high_hbm, low_hbm, in_hbm, mid_hbm, last_hbm,
    table_ref, out_ref, first_ref, middle_ref, last_ref,
    state_ref, prev_ref, high_ref, low_ref, in_ref, mid_ref, sems
):
    levels, blocks, _ = state_ref.shape
    waves = order_ref.shape[0]
    pairs = (
        (mid_hbm, mid_ref), (in_hbm, in_ref), (last_hbm, last_ref),
        (high_hbm, high_ref), (state_hbm, state_ref), (prev_hbm, prev_ref), (low_hbm, low_ref),
    )
    fetches = [
        pltpu.make_async_copy(source, target, sems.at[i]) for i, (source, target) in enumerate(pairs)
    ]
    for fetch in fetches:
        fetch.start()
    for fetch in fetches[:4]:
        fetch.wait()
    side = waves
    diagonal = lax.broadcasted_iota(jnp.int32, (side, side), 0) == lax.broadcasted_iota(
        jnp.int32, (side, side), 1
    )
    half = jnp.where(diagonal, 0.5, 0.0).astype(BF16)
    for start in range(0, mid_ref.shape[1], side):
        rows = slice(start, start + side)
        middle_ref[rows, :] = dot_nt(half, mid_ref[:, rows]).astype(BF16)
        first_ref[rows, :] = (2.0 * dot_nt(half, in_ref[:, rows])).astype(BF16)
    for part in range(2):
        rows = slice(part * waves, (part + 1) * waves)
        table_ref[rows, :] = dot(order_ref[...], high_ref[rows, :]).astype(BF16)
    for fetch in fetches[4:]:
        fetch.wait()
    parts = [
        state_ref[:, block, :] + TIME_STEP * prev_ref[:, block, :] for block in range(blocks)
    ]
    forcing = jnp.concatenate(parts, axis=1)
    blank = jnp.zeros((LANES - levels, n_lon), F32)
    high, low = split(jnp.concatenate([forcing, blank], axis=0))
    both = dot_nt(high_ref[...], jnp.concatenate([high, low], axis=0))
    natural = both[:, :LANES] + (both[:, LANES:] + dot_nt(low_ref[...], high))
    natural = (natural * (1.0 / math.sqrt(n_lon))).astype(BF16)
    for part in range(2):
        rows = slice(part * waves, (part + 1) * waves)
        out_ref[rows, :] = dot(order_ref[...], natural[rows, :]).astype(BF16)


def prepare(state, prev, order, high, low, w_in, w_mid, w_out):
    rows, n_lon = high.shape
    levels, hidden = w_in.shape
    return pl.pallas_call(
        functools.partial(prepare_kernel, n_lon),
        in_specs=[VMEM] + [HBM] * 7,
        out_specs=[VMEM] * 5,
        out_shape=[
            pltpu.HBM((rows, n_lon), BF16),
            pltpu.HBM((rows, LANES), BF16),
            jax.ShapeDtypeStruct((hidden, levels), BF16),
            jax.ShapeDtypeStruct((hidden, hidden), BF16),
            jax.ShapeDtypeStruct((levels, hidden), BF16),
        ],
        scratch_shapes=[
            pltpu.VMEM(state.shape, F32),
            pltpu.VMEM(prev.shape, F32),
            pltpu.VMEM(high.shape, BF16),
            pltpu.VMEM(low.shape, BF16),
            pltpu.VMEM(w_in.shape, BF16),
            pltpu.VMEM(w_mid.shape, BF16),
            pltpu.SemaphoreType.DMA((7,)),
        ],
        compiler_params=params(),
        cost_estimate=pl.CostEstimate(
            flops=4 * rows * n_lon * rows, bytes_accessed=12 << 20, transcendentals=0
        ),
        name="prepare",
    )(order, *in_hbm(state, prev, high, low, w_in, w_mid, w_out))


def silu(half):
    return (half + half * jnp.tanh(half)).astype(BF16)


def network_kernel(
    x_ref, first_ref, middle_ref, last_ref, table_hbm, row_hbm, out_ref, own_ref, table_ref, row_ref,
    packed_ref, done_ref, sems
):
    senders, levels, _ = out_ref.shape
    share = x_ref.shape[1] - levels
    fetches = [
        pltpu.make_async_copy(table_hbm, table_ref, sems.at[0]),
        pltpu.make_async_copy(row_hbm, row_ref, sems.at[1]),
    ]
    for fetch in fetches:
        fetch.start()
    own_ref[...] = x_ref[:, :share, :]
    heads = [x_ref[sender, share : share + 16, :].astype(F32)[:1] for sender in range(senders)]
    marked = jnp.where(jnp.concatenate(heads, axis=0) < 0.1 * MARK, 1.0, 0.0)
    marked = marked[:, :CMAX] + marked[:, CMAX:]
    lane = lax.broadcasted_iota(jnp.int32, (levels, CMAX), 1)

    def tiles(start):
        first = start // CMAX
        return [pl.ds(pl.multiple_of((first + i) * CMAX, CMAX), CMAX) for i in range(3)]

    starts = [jnp.int32(0)]
    for sender in range(senders):
        count = jnp.sum(marked[sender : sender + 1]).astype(jnp.int32)
        starts.append(starts[-1] + count)
    for sender in range(senders):
        shift = lax.rem(starts[sender], CMAX)
        places = tiles(starts[sender])
        near = pltpu.roll(x_ref[sender, share:, :CMAX].astype(F32), shift, 1)
        far = pltpu.roll(x_ref[sender, share:, CMAX:].astype(F32), shift, 1)
        packed_ref[:, places[0]] = jnp.where(lane < shift, packed_ref[:, places[0]], near)
        packed_ref[:, places[1]] = jnp.where(lane < shift, near, far)
        packed_ref[:, places[2]] = far

    def group(index, carry):
        place = pl.ds(pl.multiple_of(index * GROUP, GROUP), GROUP)
        one = silu(dot(first_ref[...], packed_ref[:, place].astype(BF16)))
        two = silu(dot(middle_ref[...], one))
        done_ref[:, place] = dot(last_ref[...], two)
        return carry

    lax.fori_loop(0, (starts[-1] + (GROUP - 1)) // GROUP, group, 0)
    for sender in range(senders):
        shift = lax.rem(starts[sender], CMAX)
        back = lax.rem(CMAX - shift, CMAX)
        near, middle, far = (pltpu.roll(done_ref[:, place], back, 1) for place in tiles(starts[sender]))
        keep = lane < CMAX - shift
        out_ref[sender, :, :CMAX] = jnp.where(keep, near, middle).astype(BF16)
        out_ref[sender, :, CMAX:] = jnp.where(keep, middle, far).astype(BF16)
    for fetch in fetches:
        fetch.wait()


def network(arrived, first_w, middle_w, last_w, table, row):
    senders, rows, width = arrived.shape
    levels, hidden = last_w.shape
    columns = -(-senders * width // GROUP) * GROUP + GROUP
    return pl.pallas_call(
        network_kernel,
        in_specs=[VMEM] * 4 + [HBM] * 2,
        out_specs=[VMEM] * 4,
        out_shape=[
            jax.ShapeDtypeStruct((senders, levels, width), BF16),
            pltpu.HBM((senders, rows - levels, width), BF16),
            pltpu.VMEM(table.shape, BF16),
            pltpu.VMEM(row.shape, BF16),
        ],
        scratch_shapes=[
            pltpu.VMEM((levels, columns), F32),
            pltpu.VMEM((levels, columns), F32),
            pltpu.SemaphoreType.DMA((2,)),
        ],
        compiler_params=params(),
        cost_estimate=pl.CostEstimate(
            flops=senders * width * hidden * (hidden + 2 * 256),
            bytes_accessed=4 << 20,
            transcendentals=senders * width * hidden,
        ),
        name="network",
    )(arrived, first_w, middle_w, last_w, *in_hbm(table, row))


def return_kernel(
    n_lon, returned_ref, table_ref, first_ref, expert_hbm, cloudy_hbm, tend_ref, out_ref,
    expert_ref, cloudy_ref, used_ref, rows_ref, sems
):
    networks, levels, _ = returned_ref.shape
    waves = first_ref.shape[0] // 2
    pairs = ((expert_hbm, expert_ref), (cloudy_hbm, cloudy_ref))
    fetches = [
        pltpu.make_async_copy(source, target, sems.at[i]) for i, (source, target) in enumerate(pairs)
    ]
    for fetch in fetches:
        fetch.start()
    lanes = lax.broadcasted_iota(jnp.int32, (levels, CMAX), 1)
    for network in range(networks):
        used_ref[network] = 0
    for fetch in fetches:
        fetch.wait()
    spans = []
    for block in range(NB_ROW):
        network = expert_ref[block]
        start = used_ref[network]
        count = cloudy_ref[block]
        used_ref[network] = start + count
        spans.append((network, start, count))
    for block, (network, start, count) in enumerate(spans):
        back = lax.rem(2 * CMAX - start, CMAX)
        near = pltpu.roll(returned_ref[network, :, :CMAX].astype(F32), back, 1)
        far = pltpu.roll(returned_ref[network, :, CMAX:].astype(F32), back, 1)
        values = jnp.where(lanes < CMAX - start, near, far)
        kept = jnp.where(lanes < count, values, 0.0)
        tend_ref[:, block * CMAX : (block + 1) * CMAX] = kept.astype(BF16)
    out = dot_nt(table_ref[...], tend_ref[...]) * (TIME_STEP / math.sqrt(n_lon))
    out = jnp.concatenate([out, jnp.zeros((out.shape[0], LANES - levels), F32)], axis=1)
    for part in range(2):
        rows = slice(part * waves, (part + 1) * waves)
        rows_ref[pl.ds(part, waves, stride=4), :] = first_ref[rows, :].astype(F32)
        rows_ref[pl.ds(2 + part, waves, stride=4), :] = out[rows]
    out_ref[...] = rows_ref[...].astype(BF16)


def return_blocks(returned, experts, cloudy, table, first):
    rows, n_lon = table.shape
    networks, levels, _ = returned.shape
    return pl.pallas_call(
        functools.partial(return_kernel, n_lon),
        in_specs=[VMEM] * 3 + [HBM] * 2,
        out_specs=[VMEM] * 2,
        out_shape=[
            pltpu.HBM((levels, n_lon), BF16),
            jax.ShapeDtypeStruct((2 * rows, LANES), BF16),
        ],
        scratch_shapes=[
            pltpu.SMEM(experts.shape, jnp.int32),
            pltpu.SMEM(cloudy.shape, jnp.int32),
            pltpu.SMEM((networks,), jnp.int32),
            pltpu.VMEM((2 * rows, LANES), F32),
            pltpu.SemaphoreType.DMA((2,)),
        ],
        compiler_params=params(),
        name="return",
    )(returned, table, first, *in_hbm(experts, cloudy))


def solve_kernel(
    scale, again, got_ref, wave_hbm, own_hbm, analysis_hbm, rate_hbm, out_ref,
    wave_ref, own_ref, analysis_ref, rate_ref, rows_ref, turn_ref, sems
):
    levels = analysis_ref.shape[0]
    networks, share, coeffs = own_ref.shape
    lats = networks * share
    pairs = (
        (wave_hbm, wave_ref), (own_hbm, own_ref), (analysis_hbm, analysis_ref), (rate_hbm, rate_ref),
    )
    fetches = [
        pltpu.make_async_copy(source, target, sems.at[i]) for i, (source, target) in enumerate(pairs)
    ]
    for fetch in fetches:
        fetch.start()
    rows_ref[...] = got_ref[...].astype(F32)
    parts = [rows_ref[pl.ds(part, lats, stride=4), :].astype(BF16) for part in range(4)]
    for fetch in fetches:
        fetch.wait()
    table = jnp.concatenate([own_ref[sender] for sender in range(networks)], axis=0)

    wave = wave_ref[lax.axis_index("dyn") * networks + lax.axis_index("phys")]
    total = (wave + lax.broadcasted_iota(jnp.int32, (levels, coeffs), 1)).astype(F32)
    rate = jnp.concatenate([rate_ref[...], jnp.zeros((1, LANES - levels), F32)], axis=1)
    rate = jnp.broadcast_to(rate, (LANES, LANES)).T[:levels]
    rate = jnp.concatenate([rate, rate], axis=1)
    inverse = 1.0 / (1.0 + TIME_STEP * (total * (total + 1.0) * scale + rate))
    blank = jnp.zeros((LANES - levels, coeffs), F32)
    gains, pulls = [], []
    for part in range(2):
        halves = [analysis_ref[:, 2 * part + half, :] for half in range(2)]
        pulled = TIME_STEP * rate * jnp.concatenate(halves, axis=1) * inverse
        gains += [inverse * (1.0 / lats), blank]
        pulls += [pulled * (1.0 / math.sqrt(coeffs)), blank]
    gain = jnp.concatenate(gains, axis=0)
    pull = jnp.concatenate(pulls, axis=0)
    real = jnp.where(wave == 0, 2.0 * again, again)
    imag = jnp.where(wave == 0, 0.0, again)
    lane = lax.broadcasted_iota(jnp.int32, (1, 2 * LANES), 1)
    regain = jnp.where(lane < LANES, real, imag)

    def there(value):
        both = dot_tn(jnp.concatenate(split(value), axis=1), table)
        return both[: 2 * LANES] + both[2 * LANES :]

    def back(value):
        both = dot_nt(table, jnp.concatenate(split(value), axis=0))
        return both[:, : 2 * LANES] + both[:, 2 * LANES :]

    spectral = dot_tn(jnp.concatenate(parts, axis=1), table)
    first = back(spectral[: 2 * LANES] * gain + pull)
    second = spectral[2 * LANES :] + there(first * regain)
    final = back(second * gain + pull)
    for part in range(2):
        turn_ref[pl.ds(part, lats, stride=2), :] = final[:, part * LANES : (part + 1) * LANES]
    out_ref[...] = turn_ref[...].astype(BF16)


def solve_twice(scale, again, got, waves, own, analysis, rate):
    rows = got.shape[0]
    return pl.pallas_call(
        functools.partial(solve_kernel, scale, again),
        in_specs=[VMEM] + [HBM] * 4,
        out_specs=VMEM,
        out_shape=jax.ShapeDtypeStruct((rows // 2, LANES), BF16),
        scratch_shapes=[
            pltpu.SMEM(waves.shape, jnp.int32),
            pltpu.VMEM(own.shape, BF16),
            pltpu.VMEM(analysis.shape, F32),
            pltpu.VMEM(rate.shape, F32),
            pltpu.VMEM((rows, LANES), F32),
            pltpu.VMEM((rows // 2, LANES), F32),
            pltpu.SemaphoreType.DMA((4,)),
        ],
        compiler_params=params(),
        name="solve",
    )(got, *in_hbm(waves, own, analysis, rate))


def synthesis_kernel(scale, home_ref, table_ref, out_ref, rows_ref):
    levels, blocks, width = out_ref.shape
    waves = home_ref.shape[0] // 2
    rows_ref[...] = home_ref[...].astype(F32)
    parts = [rows_ref[pl.ds(part, waves, stride=2), :].astype(BF16) for part in range(2)]
    grid = dot_tn(jnp.concatenate(parts, axis=0), table_ref[...]) * scale
    for block in range(blocks):
        out_ref[:, block, :] = grid[:levels, block * width : (block + 1) * width]


def synthesis(home, table, levels, scale):
    n_lon = table.shape[1]
    return pl.pallas_call(
        functools.partial(synthesis_kernel, scale),
        in_specs=[VMEM] * 2,
        out_specs=VMEM,
        out_shape=jax.ShapeDtypeStruct((levels, NB_ROW, n_lon // NB_ROW), F32),
        scratch_shapes=[pltpu.VMEM(home.shape, F32)],
        compiler_params=params(),
        name="synthesis",
    )(home, table)


def on_device(
    initial_state,
    prev_tendency,
    analysis,
    legendre,
    nudge_rate,
    band_waves,
    cloudy_count,
    expert_of,
    w_in,
    w_mid,
    w_out,
):
    levels, _, n_lon = initial_state.shape
    n_dyn = lax.axis_size("dyn")
    n_phys = lax.axis_size("phys")
    waves = band_waves.shape[0]
    coeffs = legendre.shape[3]
    lats = waves
    rows = 2 * waves
    state = initial_state.reshape(levels, NB_ROW, n_lon // NB_ROW)
    prev = prev_tendency.reshape(levels, NB_ROW, n_lon // NB_ROW)
    experts = expert_of[:, 0]

    share = lats // n_phys

    outgoing = place_blocks(experts, cloudy_count, state, legendre.reshape(n_phys, share * CAP, coeffs // CAP))
    arrived = lax.all_to_all(outgoing, "phys", split_axis=0, concat_axis=0, tiled=True)

    high, low = (jnp.asarray(part) for part in wave_table(waves, n_lon))
    chunk_waves = band_waves.reshape(n_dyn, n_phys).T.reshape(waves, 1)
    order = (chunk_waves == jnp.arange(waves, dtype=jnp.int32)[None, :]).astype(BF16)
    table, first, first_w, middle_w, last_w = prepare(
        state, prev, order, high, low, w_in[0], w_mid[0], w_out[0]
    )
    arrived, table, first, first_w, middle_w, last_w = lax.optimization_barrier(
        (arrived, table, first, first_w, middle_w, last_w)
    )
    computed, own, table, first = network(arrived, first_w, middle_w, last_w, table, first)
    returned = lax.all_to_all(computed, "phys", split_axis=0, concat_axis=0, tiled=True)

    tendency, sent = return_blocks(returned, experts, cloudy_count, table, first)
    got = lax.all_to_all(
        sent.reshape(waves, 4, LANES), ORDER, split_axis=0, concat_axis=0, tiled=True
    )
    back = solve_twice(
        1.0 / (waves * (waves + 1.0)),
        (n_lon / 2.0) / math.sqrt(waves) / math.sqrt(n_lon),
        got.reshape(4 * lats, LANES),
        band_waves,
        own,
        analysis.reshape(levels, 2 * coeffs // LANES, LANES),
        nudge_rate[None, :],
    )
    home = lax.all_to_all(
        back.reshape(lats, 2, LANES), ORDER, split_axis=0, concat_axis=0, tiled=True
    )
    final = synthesis(home.reshape(rows, LANES), table, levels, 1.0 / math.sqrt(waves))
    return (final.reshape(levels, 1, n_lon), tendency.reshape(levels, 1, n_lon))


def solution(mesh):
    in_specs = (
        P(None, ("dyn", "phys"), None),
        P(None, ("dyn", "phys"), None),
        P(None, None, ("dyn", "phys"), None),
        P("dyn", None, "phys", None),
        P(),
        P(),
        P(("dyn", "phys")),
        P(("dyn", "phys"), None),
        P("phys", None, None),
        P("phys", None, None),
        P("phys", None, None),
    )
    out_specs = (P(None, ("dyn", "phys"), None), P(None, ("dyn", "phys"), None))
    return jax.shard_map(
        on_device, mesh=mesh, in_specs=in_specs, out_specs=out_specs, check_vma=False
    )
```

```python
import functools
import math

import jax
import jax.numpy as jnp
import numpy as np
from jax import lax
from jax.experimental import pallas as pl
from jax.experimental.pallas import tpu as pltpu
from jax.sharding import PartitionSpec as P

NB_ROW = 16
CMAX = 128
CAP = 2
LANES = 128
MARK = 1e30
GROUP = 512
TIME_STEP = 0.5
ORDER = ("phys", "dyn")
VMEM = pl.BlockSpec(memory_space=pltpu.VMEM)
SMEM = pl.BlockSpec(memory_space=pltpu.SMEM)
HBM = pl.BlockSpec(memory_space=pltpu.HBM)
BF16 = jnp.bfloat16
F32 = jnp.float32


def params(mebibytes=32):
    return pltpu.CompilerParams(vmem_limit_bytes=mebibytes << 20)


def in_hbm(*arrays):
    return [pltpu.with_memory_space_constraint(array, pltpu.HBM) for array in arrays]


def wave_table(waves, n_lon):
    phases = np.arange(waves)[:, None] * np.arange(n_lon)[None, :] % n_lon
    angles = phases.astype(np.float64) * (2.0 * math.pi / n_lon)
    table = np.concatenate([np.cos(angles), -np.sin(angles)], axis=0).astype(np.float32)
    high = table.astype(jnp.bfloat16)
    low = (table - high.astype(np.float32)).astype(jnp.bfloat16)
    return high, low


def dot(a, b):
    return jnp.dot(a, b, preferred_element_type=F32)


def dot_nt(a, b):
    return lax.dot_general(a, b, (((1,), (1,)), ((), ())), preferred_element_type=F32)


def dot_tn(a, b):
    return lax.dot_general(a, b, (((0,), (0,)), ((), ())), preferred_element_type=F32)


def split(value):
    high = value.astype(BF16)
    return high, (value - high.astype(F32)).astype(BF16)


def place_kernel(
    expert_hbm, cloudy_hbm, state_hbm, legendre_hbm, out_ref,
    expert_ref, cloudy_ref, state_ref, legendre_ref, chunk_ref, used_ref, sems
):
    networks, _, width = out_ref.shape
    blocks, levels, _ = state_ref.shape
    share = legendre_ref.shape[1] // CAP
    fetches = [
        pltpu.make_async_copy(state_hbm.at[:, block, :], state_ref.at[block], sems.at[block])
        for block in range(blocks)
    ]
    pairs = ((expert_hbm, expert_ref), (cloudy_hbm, cloudy_ref), (legendre_hbm, legendre_ref))
    early = [
        pltpu.make_async_copy(source, target, sems.at[blocks + i])
        for i, (source, target) in enumerate(pairs)
    ]
    for fetch in early + fetches:
        fetch.start()
    chunk_ref[...] = jnp.full((networks, levels, width), MARK, F32)
    for network in range(networks):
        used_ref[network] = 0
    for fetch in early:
        fetch.wait()
    for network in range(networks):
        for half in range(CAP):
            part = legendre_ref[network, pl.ds(half, share, stride=CAP), :]
            out_ref[network, :share, half * CMAX : (half + 1) * CMAX] = part.astype(BF16)
    lane = lax.broadcasted_iota(jnp.int32, (levels, CMAX), 1)
    spans = []
    for block in range(blocks):
        network = expert_ref[block]
        start = used_ref[network]
        end = start + cloudy_ref[block]
        used_ref[network] = end
        spans.append((network, start, end))
    for fetch in fetches:
        fetch.wait()
    for block, (network, start, end) in enumerate(spans):
        turned = pltpu.roll(0.5 * state_ref[block], lax.rem(start, CMAX), 1)
        here = (lane >= start) & (lane < end)
        pltpu.store(chunk_ref.at[network, :, :CMAX], turned, mask=here)
        pltpu.store(chunk_ref.at[network, :, CMAX:], turned, mask=lane + CMAX < end)
    out_ref[:, share:, :] = chunk_ref[...].astype(BF16)


def place_blocks(experts, cloudy, state, legendre):
    levels, blocks, width = state.shape
    networks, share, _ = legendre.shape
    return pl.pallas_call(
        place_kernel,
        in_specs=[HBM] * 4,
        out_specs=VMEM,
        out_shape=pltpu.HBM((networks, share // CAP + levels, CAP * CMAX), BF16),
        scratch_shapes=[
            pltpu.SMEM((blocks,), jnp.int32),
            pltpu.SMEM((blocks,), jnp.int32),
            pltpu.VMEM((blocks, levels, width), F32),
            pltpu.VMEM(legendre.shape, F32),
            pltpu.VMEM((networks, levels, CAP * CMAX), F32),
            pltpu.SMEM((networks,), jnp.int32),
            pltpu.SemaphoreType.DMA((blocks + 3,)),
        ],
        compiler_params=params(),
        name="place",
    )(*in_hbm(experts, cloudy, state, legendre))


def prepare_kernel(
    n_lon, order_ref, state_hbm, prev_hbm, high_hbm, low_hbm, in_hbm, mid_hbm, last_hbm,
    wave_hbm, analysis_hbm, rate_hbm,
    table_ref, out_ref, gain_ref, pull_ref, regain_ref, first_ref, middle_ref, last_ref,
    state_ref, prev_ref, high_ref, low_ref, in_ref, mid_ref, wave_ref, analysis_ref, rate_ref, sems
):
    levels, blocks, _ = state_ref.shape
    waves = order_ref.shape[0]
    pairs = (
        (mid_hbm, mid_ref), (in_hbm, in_ref), (last_hbm, last_ref),
        (high_hbm, high_ref), (state_hbm, state_ref), (prev_hbm, prev_ref), (low_hbm, low_ref),
        (wave_hbm, wave_ref), (analysis_hbm, analysis_ref), (rate_hbm, rate_ref),
    )
    fetches = [
        pltpu.make_async_copy(source, target, sems.at[i]) for i, (source, target) in enumerate(pairs)
    ]
    for fetch in fetches:
        fetch.start()
    for fetch in fetches[:4]:
        fetch.wait()
    side = waves
    diagonal = lax.broadcasted_iota(jnp.int32, (side, side), 0) == lax.broadcasted_iota(
        jnp.int32, (side, side), 1
    )
    half = jnp.where(diagonal, 0.5, 0.0).astype(BF16)
    for start in range(0, mid_ref.shape[1], side):
        rows = slice(start, start + side)
        middle_ref[rows, :] = dot_nt(half, mid_ref[:, rows]).astype(BF16)
        first_ref[rows, :] = (2.0 * dot_nt(half, in_ref[:, rows])).astype(BF16)
    for part in range(2):
        rows = slice(part * waves, (part + 1) * waves)
        table_ref[rows, :] = dot(order_ref[...], high_ref[rows, :]).astype(BF16)
    for fetch in fetches[4:]:
        fetch.wait()
    parts = [
        state_ref[:, block, :] + TIME_STEP * prev_ref[:, block, :] for block in range(blocks)
    ]
    forcing = jnp.concatenate(parts, axis=1)
    blank = jnp.zeros((LANES - levels, n_lon), F32)
    high, low = split(jnp.concatenate([forcing, blank], axis=0))
    both = dot_nt(high_ref[...], jnp.concatenate([high, low], axis=0))
    natural = both[:, :LANES] + (both[:, LANES:] + dot_nt(low_ref[...], high))
    natural = (natural * (1.0 / math.sqrt(n_lon))).astype(BF16)
    for part in range(2):
        rows = slice(part * waves, (part + 1) * waves)
        out_ref[rows, :] = dot(order_ref[...], natural[rows, :]).astype(BF16)

    networks = lax.axis_size("phys")
    lats = waves
    coeffs = gain_ref.shape[1]
    scale = 1.0 / (waves * (waves + 1.0))
    again = (n_lon / 2.0) / math.sqrt(waves) / math.sqrt(n_lon)
    wave = wave_ref[lax.axis_index("dyn") * networks + lax.axis_index("phys")]
    total = (wave + lax.broadcasted_iota(jnp.int32, (levels, coeffs), 1)).astype(F32)
    rate = jnp.concatenate([rate_ref[...], jnp.zeros((1, LANES - levels), F32)], axis=1)
    rate = jnp.broadcast_to(rate, (LANES, LANES)).T[:levels]
    rate = jnp.concatenate([rate, rate], axis=1)
    inverse = 1.0 / (1.0 + TIME_STEP * (total * (total + 1.0) * scale + rate))
    gap = jnp.zeros((LANES - levels, coeffs), F32)
    gains, pulls = [], []
    for part in range(2):
        halves = [analysis_ref[:, 2 * part + half, :] for half in range(2)]
        pulled = TIME_STEP * rate * jnp.concatenate(halves, axis=1) * inverse
        gains += [inverse * (1.0 / math.sqrt(lats) / math.sqrt(coeffs)), gap]
        pulls += [pulled * (1.0 / math.sqrt(coeffs)), gap]
    gain_ref[...] = jnp.concatenate(gains, axis=0)
    pull_ref[...] = jnp.concatenate(pulls, axis=0)
    real = jnp.where(wave == 0, 2.0 * again, again)
    imag = jnp.where(wave == 0, 0.0, again)
    lane = lax.broadcasted_iota(jnp.int32, (1, 2 * LANES), 1)
    regain_ref[...] = jnp.where(lane < LANES, real, imag)


def prepare(state, prev, order, high, low, w_in, w_mid, w_out, waves, analysis, rate):
    rows, n_lon = high.shape
    levels, hidden = w_in.shape
    coeffs = analysis.shape[1] * analysis.shape[2] // 2
    return pl.pallas_call(
        functools.partial(prepare_kernel, n_lon),
        in_specs=[VMEM] + [HBM] * 10,
        out_specs=[VMEM] * 8,
        out_shape=[
            pltpu.HBM((rows, n_lon), BF16),
            pltpu.HBM((rows, LANES), BF16),
            pltpu.HBM((2 * LANES, coeffs), F32),
            pltpu.HBM((2 * LANES, coeffs), F32),
            pltpu.HBM((1, 2 * LANES), F32),
            jax.ShapeDtypeStruct((hidden, levels), BF16),
            jax.ShapeDtypeStruct((hidden, hidden), BF16),
            jax.ShapeDtypeStruct((levels, hidden), BF16),
        ],
        scratch_shapes=[
            pltpu.VMEM(state.shape, F32),
            pltpu.VMEM(prev.shape, F32),
            pltpu.VMEM(high.shape, BF16),
            pltpu.VMEM(low.shape, BF16),
            pltpu.VMEM(w_in.shape, BF16),
            pltpu.VMEM(w_mid.shape, BF16),
            pltpu.SMEM(waves.shape, jnp.int32),
            pltpu.VMEM(analysis.shape, F32),
            pltpu.VMEM(rate.shape, F32),
            pltpu.SemaphoreType.DMA((10,)),
        ],
        compiler_params=params(),
        cost_estimate=pl.CostEstimate(
            flops=4 * rows * n_lon * rows, bytes_accessed=12 << 20, transcendentals=0
        ),
        name="prepare",
    )(order, *in_hbm(state, prev, high, low, w_in, w_mid, w_out, waves, analysis, rate))


def silu(half):
    return (half + half * jnp.tanh(half)).astype(BF16)


def network_kernel(kept, x_ref, first_ref, middle_ref, last_ref, *refs):
    out_ref, own_ref = refs[kept : kept + 2]
    packed_ref, done_ref, sems = refs[2 * kept + 2 :]
    senders, levels, _ = out_ref.shape
    share = x_ref.shape[1] - levels
    fetches = [
        pltpu.make_async_copy(refs[i], refs[kept + 2 + i], sems.at[i]) for i in range(kept)
    ]
    for fetch in fetches:
        fetch.start()
    own_ref[...] = x_ref[:, :share, :]
    heads = [x_ref[sender, share : share + 16, :].astype(F32)[:1] for sender in range(senders)]
    marked = jnp.where(jnp.concatenate(heads, axis=0) < 0.1 * MARK, 1.0, 0.0)
    marked = marked[:, :CMAX] + marked[:, CMAX:]
    lane = lax.broadcasted_iota(jnp.int32, (levels, CMAX), 1)

    def tiles(start):
        first = start // CMAX
        return [pl.ds(pl.multiple_of((first + i) * CMAX, CMAX), CMAX) for i in range(3)]

    starts = [jnp.int32(0)]
    for sender in range(senders):
        count = jnp.sum(marked[sender : sender + 1]).astype(jnp.int32)
        starts.append(starts[-1] + count)
    for sender in range(senders):
        shift = lax.rem(starts[sender], CMAX)
        places = tiles(starts[sender])
        near = pltpu.roll(x_ref[sender, share:, :CMAX].astype(F32), shift, 1)
        far = pltpu.roll(x_ref[sender, share:, CMAX:].astype(F32), shift, 1)
        packed_ref[:, places[0]] = jnp.where(lane < shift, packed_ref[:, places[0]], near)
        packed_ref[:, places[1]] = jnp.where(lane < shift, near, far)
        packed_ref[:, places[2]] = far

    def run(place):
        one = silu(dot(first_ref[...], packed_ref[:, place].astype(BF16)))
        two = silu(dot(middle_ref[...], one))
        done_ref[:, place] = dot(last_ref[...], two)

    def pair(index, carry):
        for half in range(2):
            run(pl.ds(pl.multiple_of((2 * index + half) * GROUP, GROUP), GROUP))
        return carry

    groups = (starts[-1] + (GROUP - 1)) // GROUP
    lax.fori_loop(0, groups // 2, pair, 0)

    @pl.when(lax.rem(groups, 2) == 1)
    def _():
        run(pl.ds(pl.multiple_of((groups - 1) * GROUP, GROUP), GROUP))

    for sender in range(senders):
        shift = lax.rem(starts[sender], CMAX)
        back = lax.rem(CMAX - shift, CMAX)
        near, middle, far = (pltpu.roll(done_ref[:, place], back, 1) for place in tiles(starts[sender]))
        keep = lane < CMAX - shift
        out_ref[sender, :, :CMAX] = jnp.where(keep, near, middle).astype(BF16)
        out_ref[sender, :, CMAX:] = jnp.where(keep, middle, far).astype(BF16)
    for fetch in fetches:
        fetch.wait()


def network(arrived, first_w, middle_w, last_w, *kept):
    senders, rows, width = arrived.shape
    levels, hidden = last_w.shape
    columns = -(-senders * width // GROUP) * GROUP + GROUP
    return pl.pallas_call(
        functools.partial(network_kernel, len(kept)),
        in_specs=[VMEM] * 4 + [HBM] * len(kept),
        out_specs=[VMEM] * (2 + len(kept)),
        out_shape=[
            jax.ShapeDtypeStruct((senders, levels, width), BF16),
            pltpu.VMEM((senders, rows - levels, width), BF16),
            *[pltpu.VMEM(array.shape, array.dtype) for array in kept],
        ],
        scratch_shapes=[
            pltpu.VMEM((levels, columns), F32),
            pltpu.VMEM((levels, columns), F32),
            pltpu.SemaphoreType.DMA((len(kept),)),
        ],
        compiler_params=params(),
        cost_estimate=pl.CostEstimate(
            flops=senders * width * hidden * (hidden + 2 * 256),
            bytes_accessed=4 << 20,
            transcendentals=senders * width * hidden,
        ),
        name="network",
    )(arrived, first_w, middle_w, last_w, *in_hbm(*kept))


def return_kernel(
    n_lon, returned_ref, table_ref, first_ref, expert_ref, cloudy_ref, tend_hbm, out_ref,
    tend_ref, used_ref, rows_ref, sems
):
    networks, levels, _ = returned_ref.shape
    waves = first_ref.shape[0] // 2
    lanes = lax.broadcasted_iota(jnp.int32, (levels, CMAX), 1)
    for network in range(networks):
        used_ref[network] = 0
    spans = []
    for block in range(NB_ROW):
        network = expert_ref[block]
        start = used_ref[network]
        count = cloudy_ref[block]
        used_ref[network] = start + count
        spans.append((network, start, count))
    for block, (network, start, count) in enumerate(spans):
        back = lax.rem(2 * CMAX - start, CMAX)
        near = pltpu.roll(returned_ref[network, :, :CMAX].astype(F32), back, 1)
        far = pltpu.roll(returned_ref[network, :, CMAX:].astype(F32), back, 1)
        values = jnp.where(lanes < CMAX - start, near, far)
        kept = jnp.where(lanes < count, values, 0.0)
        tend_ref[:, block * CMAX : (block + 1) * CMAX] = kept.astype(BF16)
    leave = pltpu.make_async_copy(tend_ref, tend_hbm, sems.at[0])
    leave.start()
    out = dot_nt(table_ref[...], tend_ref[...]) * (TIME_STEP / math.sqrt(n_lon))
    out = jnp.concatenate([out, jnp.zeros((out.shape[0], LANES - levels), F32)], axis=1)
    for part in range(2):
        rows = slice(part * waves, (part + 1) * waves)
        rows_ref[pl.ds(part, waves, stride=4), :] = first_ref[rows, :].astype(F32)
        rows_ref[pl.ds(2 + part, waves, stride=4), :] = out[rows]
    out_ref[...] = rows_ref[...].astype(BF16)
    leave.wait()


def return_blocks(returned, experts, cloudy, table, first):
    rows, n_lon = table.shape
    networks, levels, _ = returned.shape
    return pl.pallas_call(
        functools.partial(return_kernel, n_lon),
        in_specs=[VMEM] * 3 + [SMEM] * 2,
        out_specs=[HBM, VMEM],
        out_shape=[
            pltpu.HBM((levels, n_lon), BF16),
            jax.ShapeDtypeStruct((2 * rows, LANES), BF16),
        ],
        scratch_shapes=[
            pltpu.VMEM((levels, n_lon), BF16),
            pltpu.SMEM((networks,), jnp.int32),
            pltpu.VMEM((2 * rows, LANES), F32),
            pltpu.SemaphoreType.DMA((1,)),
        ],
        compiler_params=params(),
        name="return",
    )(returned, table, first, experts, cloudy)


def solve_kernel(got_ref, own_ref, gain_ref, pull_ref, regain_ref, out_ref, rows_ref, turn_ref):
    networks, share, _ = own_ref.shape
    lats = networks * share
    rows_ref[...] = got_ref[...].astype(F32)
    parts = [rows_ref[pl.ds(part, lats, stride=4), :].astype(BF16) for part in range(4)]
    table = jnp.concatenate([own_ref[sender] for sender in range(networks)], axis=0)
    gain = gain_ref[...]
    pull = pull_ref[...]
    regain = regain_ref[...]

    def there(value):
        both = dot_tn(jnp.concatenate(split(value), axis=1), table)
        return both[: 2 * LANES] + both[2 * LANES :]

    def back(value):
        both = dot_nt(table, jnp.concatenate(split(value), axis=0))
        return both[:, : 2 * LANES] + both[:, 2 * LANES :]

    spectral = dot_tn(jnp.concatenate(parts, axis=1), table)
    first = back(spectral[: 2 * LANES] * gain + pull)
    second = spectral[2 * LANES :] + there(first * regain)
    final = back(second * gain + pull)
    for part in range(2):
        turn_ref[pl.ds(part, lats, stride=2), :] = final[:, part * LANES : (part + 1) * LANES]
    out_ref[...] = turn_ref[...].astype(BF16)


def solve_twice(got, own, gain, pull, regain):
    rows = got.shape[0]
    return pl.pallas_call(
        solve_kernel,
        in_specs=[VMEM] * 5,
        out_specs=VMEM,
        out_shape=jax.ShapeDtypeStruct((rows // 2, LANES), BF16),
        scratch_shapes=[pltpu.VMEM((rows, LANES), F32), pltpu.VMEM((rows // 2, LANES), F32)],
        compiler_params=params(),
        name="solve",
    )(got, own, gain, pull, regain)


def synthesis_kernel(scale, home_ref, table_ref, out_hbm, rows_ref, out_ref, sems):
    levels, blocks, width = out_ref.shape
    waves = home_ref.shape[0] // 2
    rows_ref[...] = home_ref[...].astype(F32)
    parts = [rows_ref[pl.ds(part, waves, stride=2), :].astype(BF16) for part in range(2)]
    spectrum = jnp.concatenate(parts, axis=0).T
    cut = 4
    copies = []
    for start in range(0, blocks, cut):
        grid = dot(spectrum, table_ref[:, start * width : (start + cut) * width]) * scale
        for block in range(cut):
            out_ref[:, start + block, :] = grid[:levels, block * width : (block + 1) * width]
        place = slice(start, start + cut)
        copies.append(
            pltpu.make_async_copy(out_ref.at[:, place, :], out_hbm.at[:, place, :], sems.at[start // cut])
        )
        copies[-1].start()
    for copy in copies:
        copy.wait()


def synthesis(home, table, levels, scale):
    n_lon = table.shape[1]
    shape = (levels, NB_ROW, n_lon // NB_ROW)
    return pl.pallas_call(
        functools.partial(synthesis_kernel, scale),
        in_specs=[VMEM] * 2,
        out_specs=HBM,
        out_shape=pltpu.HBM(shape, F32),
        scratch_shapes=[
            pltpu.VMEM(home.shape, F32),
            pltpu.VMEM(shape, F32),
            pltpu.SemaphoreType.DMA((NB_ROW // 4,)),
        ],
        compiler_params=params(),
        name="synthesis",
    )(home, table)


def on_device(
    initial_state,
    prev_tendency,
    analysis,
    legendre,
    nudge_rate,
    band_waves,
    cloudy_count,
    expert_of,
    w_in,
    w_mid,
    w_out,
):
    levels, _, n_lon = initial_state.shape
    n_dyn = lax.axis_size("dyn")
    n_phys = lax.axis_size("phys")
    waves = band_waves.shape[0]
    coeffs = legendre.shape[3]
    lats = waves
    rows = 2 * waves
    state = initial_state.reshape(levels, NB_ROW, n_lon // NB_ROW)
    prev = prev_tendency.reshape(levels, NB_ROW, n_lon // NB_ROW)
    experts = expert_of[:, 0]

    share = lats // n_phys

    outgoing = place_blocks(experts, cloudy_count, state, legendre.reshape(n_phys, share * CAP, coeffs // CAP))
    arrived = lax.all_to_all(outgoing, "phys", split_axis=0, concat_axis=0, tiled=True)

    high, low = (jnp.asarray(part) for part in wave_table(waves, n_lon))
    chunk_waves = band_waves.reshape(n_dyn, n_phys).T.reshape(waves, 1)
    order = (chunk_waves == jnp.arange(waves, dtype=jnp.int32)[None, :]).astype(BF16)
    table, first, gain, pull, regain, first_w, middle_w, last_w = prepare(
        state,
        prev,
        order,
        high,
        low,
        w_in[0],
        w_mid[0],
        w_out[0],
        band_waves,
        analysis.reshape(levels, 2 * coeffs // LANES, LANES),
        nudge_rate[None, :],
    )
    arrived, first_w, middle_w, last_w, *kept = lax.optimization_barrier(
        (arrived, first_w, middle_w, last_w, table, first, gain, pull, regain)
    )
    computed, own, table, first, gain, pull, regain = network(
        arrived, first_w, middle_w, last_w, *kept
    )
    returned = lax.all_to_all(computed, "phys", split_axis=0, concat_axis=0, tiled=True)

    tendency, sent = return_blocks(returned, experts, cloudy_count, table, first)
    got = lax.all_to_all(
        sent.reshape(waves, 4, LANES), ORDER, split_axis=0, concat_axis=0, tiled=True
    )
    back = solve_twice(got.reshape(4 * lats, LANES), own, gain, pull, regain)
    home = lax.all_to_all(
        back.reshape(lats, 2, LANES), ORDER, split_axis=0, concat_axis=0, tiled=True
    )
    final = synthesis(home.reshape(rows, LANES), table, levels, 1.0 / math.sqrt(waves))
    return (final.reshape(levels, 1, n_lon), tendency.reshape(levels, 1, n_lon))


def solution(mesh):
    in_specs = (
        P(None, ("dyn", "phys"), None),
        P(None, ("dyn", "phys"), None),
        P(None, None, ("dyn", "phys"), None),
        P("dyn", None, "phys", None),
        P(),
        P(),
        P(("dyn", "phys")),
        P(("dyn", "phys"), None),
        P("phys", None, None),
        P("phys", None, None),
        P("phys", None, None),
    )
    out_specs = (P(None, ("dyn", "phys"), None), P(None, ("dyn", "phys"), None))
    return jax.shard_map(
        on_device, mesh=mesh, in_specs=in_specs, out_specs=out_specs, check_vma=False
    )
```

```python
import functools
import math

import jax
import jax.numpy as jnp
import numpy as np
from jax import lax
from jax.experimental import pallas as pl
from jax.experimental.pallas import tpu as pltpu
from jax.sharding import PartitionSpec as P

NB_ROW = 16
CMAX = 128
CAP = 2
LANES = 128
MARK = 1e30
GROUP = 512
TIME_STEP = 0.5
ORDER = ("phys", "dyn")
VMEM = pl.BlockSpec(memory_space=pltpu.VMEM)
SMEM = pl.BlockSpec(memory_space=pltpu.SMEM)
HBM = pl.BlockSpec(memory_space=pltpu.HBM)
BF16 = jnp.bfloat16
F32 = jnp.float32


def params(mebibytes=32):
    return pltpu.CompilerParams(vmem_limit_bytes=mebibytes << 20)


def in_hbm(*arrays):
    return [pltpu.with_memory_space_constraint(array, pltpu.HBM) for array in arrays]


def wave_table(waves, n_lon):
    phases = np.arange(waves)[:, None] * np.arange(n_lon)[None, :] % n_lon
    angles = phases.astype(np.float64) * (2.0 * math.pi / n_lon)
    table = np.concatenate([np.cos(angles), -np.sin(angles)], axis=0).astype(np.float32)
    high = table.astype(jnp.bfloat16)
    low = (table - high.astype(np.float32)).astype(jnp.bfloat16)
    return high, low


def dot(a, b):
    return jnp.dot(a, b, preferred_element_type=F32)


def dot_nt(a, b):
    return lax.dot_general(a, b, (((1,), (1,)), ((), ())), preferred_element_type=F32)


def dot_tn(a, b):
    return lax.dot_general(a, b, (((0,), (0,)), ((), ())), preferred_element_type=F32)


def split(value):
    high = value.astype(BF16)
    return high, (value - high.astype(F32)).astype(BF16)


def place_kernel(
    expert_hbm, cloudy_hbm, state_hbm, legendre_hbm, out_ref,
    expert_ref, cloudy_ref, state_ref, legendre_ref, chunk_ref, used_ref, sems
):
    networks, _, width = out_ref.shape
    blocks, levels, _ = state_ref.shape
    share = legendre_ref.shape[1] // CAP
    fetches = [
        pltpu.make_async_copy(state_hbm.at[:, block, :], state_ref.at[block], sems.at[block])
        for block in range(blocks)
    ]
    pairs = ((expert_hbm, expert_ref), (cloudy_hbm, cloudy_ref), (legendre_hbm, legendre_ref))
    early = [
        pltpu.make_async_copy(source, target, sems.at[blocks + i])
        for i, (source, target) in enumerate(pairs)
    ]
    for fetch in early + fetches:
        fetch.start()
    chunk_ref[...] = jnp.full((networks, levels, width), MARK, F32)
    for network in range(networks):
        used_ref[network] = 0
    for fetch in early:
        fetch.wait()
    for network in range(networks):
        for half in range(CAP):
            part = legendre_ref[network, pl.ds(half, share, stride=CAP), :]
            out_ref[network, :share, half * CMAX : (half + 1) * CMAX] = part.astype(BF16)
    lane = lax.broadcasted_iota(jnp.int32, (levels, CMAX), 1)
    spans = []
    for block in range(blocks):
        network = expert_ref[block]
        start = used_ref[network]
        end = start + cloudy_ref[block]
        used_ref[network] = end
        spans.append((network, start, end))
    for fetch in fetches:
        fetch.wait()
    for block, (network, start, end) in enumerate(spans):
        turned = pltpu.roll(0.5 * state_ref[block], lax.rem(start, CMAX), 1)
        here = (lane >= start) & (lane < end)
        pltpu.store(chunk_ref.at[network, :, :CMAX], turned, mask=here)
        pltpu.store(chunk_ref.at[network, :, CMAX:], turned, mask=lane + CMAX < end)
    out_ref[:, share:, :] = chunk_ref[...].astype(BF16)


def place_blocks(experts, cloudy, state, legendre):
    levels, blocks, width = state.shape
    networks, share, _ = legendre.shape
    return pl.pallas_call(
        place_kernel,
        in_specs=[HBM] * 4,
        out_specs=VMEM,
        out_shape=pltpu.HBM((networks, share // CAP + levels, CAP * CMAX), BF16),
        scratch_shapes=[
            pltpu.SMEM((blocks,), jnp.int32),
            pltpu.SMEM((blocks,), jnp.int32),
            pltpu.VMEM((blocks, levels, width), F32),
            pltpu.VMEM(legendre.shape, F32),
            pltpu.VMEM((networks, levels, CAP * CMAX), F32),
            pltpu.SMEM((networks,), jnp.int32),
            pltpu.SemaphoreType.DMA((blocks + 3,)),
        ],
        compiler_params=params(),
        name="place",
    )(*in_hbm(experts, cloudy, state, legendre))


def prepare_kernel(
    n_lon, order_ref, state_hbm, prev_hbm, high_hbm, low_hbm, in_hbm, mid_hbm, last_hbm,
    wave_hbm, analysis_hbm, rate_hbm,
    table_ref, out_ref, gain_ref, pull_ref, regain_ref, first_ref, middle_ref, last_ref,
    state_ref, prev_ref, high_ref, low_ref, in_ref, mid_ref, wave_ref, analysis_ref, rate_ref, sems
):
    levels, blocks, _ = state_ref.shape
    waves = order_ref.shape[0]
    pairs = (
        (mid_hbm, mid_ref), (in_hbm, in_ref), (last_hbm, last_ref),
        (high_hbm, high_ref), (state_hbm, state_ref), (prev_hbm, prev_ref), (low_hbm, low_ref),
        (wave_hbm, wave_ref), (analysis_hbm, analysis_ref), (rate_hbm, rate_ref),
    )
    fetches = [
        pltpu.make_async_copy(source, target, sems.at[i]) for i, (source, target) in enumerate(pairs)
    ]
    for fetch in fetches:
        fetch.start()
    for fetch in fetches[:4]:
        fetch.wait()
    side = waves
    diagonal = lax.broadcasted_iota(jnp.int32, (side, side), 0) == lax.broadcasted_iota(
        jnp.int32, (side, side), 1
    )
    half = jnp.where(diagonal, 0.5, 0.0).astype(BF16)
    for start in range(0, mid_ref.shape[1], side):
        rows = slice(start, start + side)
        middle_ref[rows, :] = dot_nt(half, mid_ref[:, rows]).astype(BF16)
        first_ref[rows, :] = (2.0 * dot_nt(half, in_ref[:, rows])).astype(BF16)
    for part in range(2):
        rows = slice(part * waves, (part + 1) * waves)
        table_ref[rows, :] = dot(order_ref[...], high_ref[rows, :]).astype(BF16)
    for fetch in fetches[4:]:
        fetch.wait()
    parts = [
        state_ref[:, block, :] + TIME_STEP * prev_ref[:, block, :] for block in range(blocks)
    ]
    forcing = jnp.concatenate(parts, axis=1)
    blank = jnp.zeros((LANES - levels, n_lon), F32)
    high, low = split(jnp.concatenate([forcing, blank], axis=0))
    both = dot_nt(high_ref[...], jnp.concatenate([high, low], axis=0))
    natural = both[:, :LANES] + (both[:, LANES:] + dot_nt(low_ref[...], high))
    natural = (natural * (1.0 / math.sqrt(n_lon))).astype(BF16)
    for part in range(2):
        rows = slice(part * waves, (part + 1) * waves)
        out_ref[rows, :] = dot(order_ref[...], natural[rows, :]).astype(BF16)

    networks = lax.axis_size("phys")
    lats = waves
    coeffs = gain_ref.shape[1]
    scale = 1.0 / (waves * (waves + 1.0))
    again = (n_lon / 2.0) / math.sqrt(waves) / math.sqrt(n_lon)
    wave = wave_ref[lax.axis_index("dyn") * networks + lax.axis_index("phys")]
    total = (wave + lax.broadcasted_iota(jnp.int32, (levels, coeffs), 1)).astype(F32)
    rate = jnp.concatenate([rate_ref[...], jnp.zeros((1, LANES - levels), F32)], axis=1)
    rate = jnp.broadcast_to(rate, (LANES, LANES)).T[:levels]
    rate = jnp.concatenate([rate, rate], axis=1)
    inverse = 1.0 / (1.0 + TIME_STEP * (total * (total + 1.0) * scale + rate))
    gap = jnp.zeros((LANES - levels, coeffs), F32)
    gains, pulls = [], []
    for part in range(2):
        halves = [analysis_ref[:, 2 * part + half, :] for half in range(2)]
        pulled = TIME_STEP * rate * jnp.concatenate(halves, axis=1) * inverse
        gains += [inverse * (1.0 / math.sqrt(lats) / math.sqrt(coeffs)), gap]
        pulls += [pulled * (1.0 / math.sqrt(coeffs)), gap]
    gain_ref[...] = jnp.concatenate(gains, axis=0)
    pull_ref[...] = jnp.concatenate(pulls, axis=0)
    real = jnp.where(wave == 0, 2.0 * again, again)
    imag = jnp.where(wave == 0, 0.0, again)
    lane = lax.broadcasted_iota(jnp.int32, (1, 2 * LANES), 1)
    regain_ref[...] = jnp.where(lane < LANES, real, imag)


def prepare(state, prev, order, high, low, w_in, w_mid, w_out, waves, analysis, rate):
    rows, n_lon = high.shape
    levels, hidden = w_in.shape
    coeffs = analysis.shape[1] * analysis.shape[2] // 2
    return pl.pallas_call(
        functools.partial(prepare_kernel, n_lon),
        in_specs=[VMEM] + [HBM] * 10,
        out_specs=[VMEM] * 8,
        out_shape=[
            pltpu.HBM((rows, n_lon), BF16),
            pltpu.HBM((rows, LANES), BF16),
            pltpu.HBM((2 * LANES, coeffs), F32),
            pltpu.HBM((2 * LANES, coeffs), F32),
            pltpu.HBM((1, 2 * LANES), F32),
            jax.ShapeDtypeStruct((hidden, levels), BF16),
            jax.ShapeDtypeStruct((hidden, hidden), BF16),
            jax.ShapeDtypeStruct((levels, hidden), BF16),
        ],
        scratch_shapes=[
            pltpu.VMEM(state.shape, F32),
            pltpu.VMEM(prev.shape, F32),
            pltpu.VMEM(high.shape, BF16),
            pltpu.VMEM(low.shape, BF16),
            pltpu.VMEM(w_in.shape, BF16),
            pltpu.VMEM(w_mid.shape, BF16),
            pltpu.SMEM(waves.shape, jnp.int32),
            pltpu.VMEM(analysis.shape, F32),
            pltpu.VMEM(rate.shape, F32),
            pltpu.SemaphoreType.DMA((10,)),
        ],
        compiler_params=params(),
        cost_estimate=pl.CostEstimate(
            flops=4 * rows * n_lon * rows, bytes_accessed=12 << 20, transcendentals=0
        ),
        name="prepare",
    )(order, *in_hbm(state, prev, high, low, w_in, w_mid, w_out, waves, analysis, rate))


def silu(half):
    return (half + half * jnp.tanh(half)).astype(BF16)


def network_kernel(kept, x_ref, first_ref, middle_ref, last_ref, *refs):
    out_ref, own_ref = refs[kept : kept + 2]
    packed_ref, done_ref, sems = refs[2 * kept + 2 :]
    senders, levels, _ = out_ref.shape
    share = x_ref.shape[1] - levels
    fetches = [
        pltpu.make_async_copy(refs[i], refs[kept + 2 + i], sems.at[i]) for i in range(kept)
    ]
    for fetch in fetches:
        fetch.start()
    own_ref[...] = x_ref[:, :share, :]
    heads = [x_ref[sender, share : share + 16, :].astype(F32)[:1] for sender in range(senders)]
    marked = jnp.where(jnp.concatenate(heads, axis=0) < 0.1 * MARK, 1.0, 0.0)
    marked = marked[:, :CMAX] + marked[:, CMAX:]
    lane = lax.broadcasted_iota(jnp.int32, (levels, CMAX), 1)

    def tiles(start):
        first = start // CMAX
        return [pl.ds(pl.multiple_of((first + i) * CMAX, CMAX), CMAX) for i in range(3)]

    starts = [jnp.int32(0)]
    for sender in range(senders):
        count = jnp.sum(marked[sender : sender + 1]).astype(jnp.int32)
        starts.append(starts[-1] + count)
    for sender in range(senders):
        shift = lax.rem(starts[sender], CMAX)
        places = tiles(starts[sender])
        near = pltpu.roll(x_ref[sender, share:, :CMAX].astype(F32), shift, 1)
        far = pltpu.roll(x_ref[sender, share:, CMAX:].astype(F32), shift, 1)
        packed_ref[:, places[0]] = jnp.where(lane < shift, packed_ref[:, places[0]], near)
        packed_ref[:, places[1]] = jnp.where(lane < shift, near, far)
        packed_ref[:, places[2]] = far

    def run(start, width, step):
        place = pl.ds(pl.multiple_of(start, width), width)
        columns = packed_ref[:, place].astype(BF16)
        cuts = [slice(row, row + step) for row in range(0, middle_ref.shape[0], step)]
        one = jnp.concatenate([silu(dot(first_ref[cut, :], columns)) for cut in cuts], axis=0)
        two = jnp.concatenate([silu(dot(middle_ref[cut, :], one)) for cut in cuts], axis=0)
        done_ref[:, place] = dot(last_ref[...], two)

    def four(index, carry):
        for i in range(4):
            run((4 * index + i) * GROUP, GROUP, middle_ref.shape[0])
        return carry

    def single(index, carry):
        run(index * GROUP, GROUP, middle_ref.shape[0])
        return carry

    half = GROUP // 2
    halves = (starts[-1] + (half - 1)) // half
    groups = halves // 2
    lax.fori_loop(0, groups // 4, four, 0)
    lax.fori_loop(groups // 4 * 4, groups, single, 0)

    @pl.when(lax.rem(halves, 2) == 1)
    def _():
        run((halves - 1) * half, half, half)

    for sender in range(senders):
        shift = lax.rem(starts[sender], CMAX)
        back = lax.rem(CMAX - shift, CMAX)
        near, middle, far = (pltpu.roll(done_ref[:, place], back, 1) for place in tiles(starts[sender]))
        keep = lane < CMAX - shift
        out_ref[sender, :, :CMAX] = jnp.where(keep, near, middle).astype(BF16)
        out_ref[sender, :, CMAX:] = jnp.where(keep, middle, far).astype(BF16)
    for fetch in fetches:
        fetch.wait()


def network(arrived, first_w, middle_w, last_w, *kept):
    senders, rows, width = arrived.shape
    levels, hidden = last_w.shape
    columns = -(-senders * width // GROUP) * GROUP + GROUP
    return pl.pallas_call(
        functools.partial(network_kernel, len(kept)),
        in_specs=[VMEM] * 4 + [HBM] * len(kept),
        out_specs=[VMEM] * (2 + len(kept)),
        out_shape=[
            jax.ShapeDtypeStruct((senders, levels, width), BF16),
            pltpu.VMEM((senders, rows - levels, width), BF16),
            *[pltpu.VMEM(array.shape, array.dtype) for array in kept],
        ],
        scratch_shapes=[
            pltpu.VMEM((levels, columns), F32),
            pltpu.VMEM((levels, columns), F32),
            pltpu.SemaphoreType.DMA((len(kept),)),
        ],
        compiler_params=params(),
        cost_estimate=pl.CostEstimate(
            flops=senders * width * hidden * (hidden + 2 * 256),
            bytes_accessed=4 << 20,
            transcendentals=senders * width * hidden,
        ),
        name="network",
    )(arrived, first_w, middle_w, last_w, *in_hbm(*kept))


def return_kernel(
    n_lon, returned_ref, table_ref, first_ref, expert_ref, cloudy_ref, tend_hbm, out_ref,
    tend_ref, used_ref, rows_ref, sems
):
    networks, levels, _ = returned_ref.shape
    waves = first_ref.shape[0] // 2
    lanes = lax.broadcasted_iota(jnp.int32, (levels, CMAX), 1)
    for network in range(networks):
        used_ref[network] = 0
    spans = []
    for block in range(NB_ROW):
        network = expert_ref[block]
        start = used_ref[network]
        count = cloudy_ref[block]
        used_ref[network] = start + count
        spans.append((network, start, count))
    for block, (network, start, count) in enumerate(spans):
        back = lax.rem(2 * CMAX - start, CMAX)
        near = pltpu.roll(returned_ref[network, :, :CMAX].astype(F32), back, 1)
        far = pltpu.roll(returned_ref[network, :, CMAX:].astype(F32), back, 1)
        values = jnp.where(lanes < CMAX - start, near, far)
        kept = jnp.where(lanes < count, values, 0.0)
        tend_ref[:, block * CMAX : (block + 1) * CMAX] = kept.astype(BF16)
    leave = pltpu.make_async_copy(tend_ref, tend_hbm, sems.at[0])
    leave.start()
    out = dot_nt(table_ref[...], tend_ref[...]) * (TIME_STEP / math.sqrt(n_lon))
    out = jnp.concatenate([out, jnp.zeros((out.shape[0], LANES - levels), F32)], axis=1)
    for part in range(2):
        rows = slice(part * waves, (part + 1) * waves)
        rows_ref[pl.ds(part, waves, stride=4), :] = first_ref[rows, :].astype(F32)
        rows_ref[pl.ds(2 + part, waves, stride=4), :] = out[rows]
    out_ref[...] = rows_ref[...].astype(BF16)
    leave.wait()


def return_blocks(returned, experts, cloudy, table, first):
    rows, n_lon = table.shape
    networks, levels, _ = returned.shape
    return pl.pallas_call(
        functools.partial(return_kernel, n_lon),
        in_specs=[VMEM] * 3 + [SMEM] * 2,
        out_specs=[HBM, VMEM],
        out_shape=[
            pltpu.HBM((levels, n_lon), BF16),
            jax.ShapeDtypeStruct((2 * rows, LANES), BF16),
        ],
        scratch_shapes=[
            pltpu.VMEM((levels, n_lon), BF16),
            pltpu.SMEM((networks,), jnp.int32),
            pltpu.VMEM((2 * rows, LANES), F32),
            pltpu.SemaphoreType.DMA((1,)),
        ],
        compiler_params=params(),
        name="return",
    )(returned, table, first, experts, cloudy)


def solve_kernel(got_ref, own_ref, gain_ref, pull_ref, regain_ref, out_ref, rows_ref, turn_ref):
    networks, share, _ = own_ref.shape
    lats = networks * share
    rows_ref[...] = got_ref[...].astype(F32)
    parts = [rows_ref[pl.ds(part, lats, stride=4), :].astype(BF16) for part in range(4)]
    table = jnp.concatenate([own_ref[sender] for sender in range(networks)], axis=0)
    gain = gain_ref[...]
    pull = pull_ref[...]
    regain = regain_ref[...]

    def there(value):
        both = dot_tn(jnp.concatenate(split(value), axis=1), table)
        return both[: 2 * LANES] + both[2 * LANES :]

    def back(value):
        both = dot_nt(table, jnp.concatenate(split(value), axis=0))
        return both[:, : 2 * LANES] + both[:, 2 * LANES :]

    spectral = dot_tn(jnp.concatenate(parts, axis=1), table)
    first = back(spectral[: 2 * LANES] * gain + pull)
    second = spectral[2 * LANES :] + there(first * regain)
    final = back(second * gain + pull)
    for part in range(2):
        turn_ref[pl.ds(part, lats, stride=2), :] = final[:, part * LANES : (part + 1) * LANES]
    out_ref[...] = turn_ref[...].astype(BF16)


def solve_twice(got, own, gain, pull, regain):
    rows = got.shape[0]
    return pl.pallas_call(
        solve_kernel,
        in_specs=[VMEM] * 5,
        out_specs=VMEM,
        out_shape=jax.ShapeDtypeStruct((rows // 2, LANES), BF16),
        scratch_shapes=[pltpu.VMEM((rows, LANES), F32), pltpu.VMEM((rows // 2, LANES), F32)],
        compiler_params=params(),
        name="solve",
    )(got, own, gain, pull, regain)


def synthesis_kernel(scale, home_ref, table_ref, out_hbm, rows_ref, out_ref, sems):
    levels, blocks, width = out_ref.shape
    waves = home_ref.shape[0] // 2
    rows_ref[...] = home_ref[...].astype(F32)
    parts = [rows_ref[pl.ds(part, waves, stride=2), :].astype(BF16) for part in range(2)]
    spectrum = jnp.concatenate(parts, axis=0).T
    cut = 4
    copies = []
    for start in range(0, blocks, cut):
        grid = dot(spectrum, table_ref[:, start * width : (start + cut) * width]) * scale
        for block in range(cut):
            out_ref[:, start + block, :] = grid[:levels, block * width : (block + 1) * width]
        place = slice(start, start + cut)
        copies.append(
            pltpu.make_async_copy(out_ref.at[:, place, :], out_hbm.at[:, place, :], sems.at[start // cut])
        )
        copies[-1].start()
    for copy in copies:
        copy.wait()


def synthesis(home, table, levels, scale):
    n_lon = table.shape[1]
    shape = (levels, NB_ROW, n_lon // NB_ROW)
    return pl.pallas_call(
        functools.partial(synthesis_kernel, scale),
        in_specs=[VMEM] * 2,
        out_specs=HBM,
        out_shape=pltpu.HBM(shape, F32),
        scratch_shapes=[
            pltpu.VMEM(home.shape, F32),
            pltpu.VMEM(shape, F32),
            pltpu.SemaphoreType.DMA((NB_ROW // 4,)),
        ],
        compiler_params=params(),
        name="synthesis",
    )(home, table)


def on_device(
    initial_state,
    prev_tendency,
    analysis,
    legendre,
    nudge_rate,
    band_waves,
    cloudy_count,
    expert_of,
    w_in,
    w_mid,
    w_out,
):
    levels, _, n_lon = initial_state.shape
    n_dyn = lax.axis_size("dyn")
    n_phys = lax.axis_size("phys")
    waves = band_waves.shape[0]
    coeffs = legendre.shape[3]
    lats = waves
    rows = 2 * waves
    state = initial_state.reshape(levels, NB_ROW, n_lon // NB_ROW)
    prev = prev_tendency.reshape(levels, NB_ROW, n_lon // NB_ROW)
    experts = expert_of[:, 0]

    share = lats // n_phys

    outgoing = place_blocks(experts, cloudy_count, state, legendre.reshape(n_phys, share * CAP, coeffs // CAP))
    arrived = lax.all_to_all(outgoing, "phys", split_axis=0, concat_axis=0, tiled=True)

    high, low = (jnp.asarray(part) for part in wave_table(waves, n_lon))
    chunk_waves = band_waves.reshape(n_dyn, n_phys).T.reshape(waves, 1)
    order = (chunk_waves == jnp.arange(waves, dtype=jnp.int32)[None, :]).astype(BF16)
    table, first, gain, pull, regain, first_w, middle_w, last_w = prepare(
        state,
        prev,
        order,
        high,
        low,
        w_in[0],
        w_mid[0],
        w_out[0],
        band_waves,
        analysis.reshape(levels, 2 * coeffs // LANES, LANES),
        nudge_rate[None, :],
    )
    arrived, first_w, middle_w, last_w, *kept = lax.optimization_barrier(
        (arrived, first_w, middle_w, last_w, table, first, gain, pull, regain)
    )
    computed, own, table, first, gain, pull, regain = network(
        arrived, first_w, middle_w, last_w, *kept
    )
    returned = lax.all_to_all(computed, "phys", split_axis=0, concat_axis=0, tiled=True)

    tendency, sent = return_blocks(returned, experts, cloudy_count, table, first)
    got = lax.all_to_all(
        sent.reshape(waves, 4, LANES), ORDER, split_axis=0, concat_axis=0, tiled=True
    )
    back = solve_twice(got.reshape(4 * lats, LANES), own, gain, pull, regain)
    home = lax.all_to_all(
        back.reshape(lats, 2, LANES), ORDER, split_axis=0, concat_axis=0, tiled=True
    )
    final = synthesis(home.reshape(rows, LANES), table, levels, 1.0 / math.sqrt(waves))
    return (final.reshape(levels, 1, n_lon), tendency.reshape(levels, 1, n_lon))


def solution(mesh):
    in_specs = (
        P(None, ("dyn", "phys"), None),
        P(None, ("dyn", "phys"), None),
        P(None, None, ("dyn", "phys"), None),
        P("dyn", None, "phys", None),
        P(),
        P(),
        P(("dyn", "phys")),
        P(("dyn", "phys"), None),
        P("phys", None, None),
        P("phys", None, None),
        P("phys", None, None),
    )
    out_specs = (P(None, ("dyn", "phys"), None), P(None, ("dyn", "phys"), None))
    return jax.shard_map(
        on_device, mesh=mesh, in_specs=in_specs, out_specs=out_specs, check_vma=False
    )
```

```python
import functools
import math

import jax
import jax.numpy as jnp
import numpy as np
from jax import lax
from jax.experimental import pallas as pl
from jax.experimental.pallas import tpu as pltpu
from jax.sharding import PartitionSpec as P

NB_ROW = 16
CMAX = 128
CAP = 2
LANES = 128
MARK = 1e30
GROUP = 512
TIME_STEP = 0.5
ORDER = ("phys", "dyn")
VMEM = pl.BlockSpec(memory_space=pltpu.VMEM)
SMEM = pl.BlockSpec(memory_space=pltpu.SMEM)
HBM = pl.BlockSpec(memory_space=pltpu.HBM)
BF16 = jnp.bfloat16
F32 = jnp.float32


def params(mebibytes=32):
    return pltpu.CompilerParams(vmem_limit_bytes=mebibytes << 20)


def in_hbm(*arrays):
    return [pltpu.with_memory_space_constraint(array, pltpu.HBM) for array in arrays]


def wave_table(waves, n_lon):
    phases = np.arange(waves)[:, None] * np.arange(n_lon)[None, :] % n_lon
    angles = phases.astype(np.float64) * (2.0 * math.pi / n_lon)
    table = np.concatenate([np.cos(angles), -np.sin(angles)], axis=0).astype(np.float32)
    high = table.astype(jnp.bfloat16)
    low = (table - high.astype(np.float32)).astype(jnp.bfloat16)
    return high, low


def dot(a, b):
    return jnp.dot(a, b, preferred_element_type=F32)


def dot_nt(a, b):
    return lax.dot_general(a, b, (((1,), (1,)), ((), ())), preferred_element_type=F32)


def dot_tn(a, b):
    return lax.dot_general(a, b, (((0,), (0,)), ((), ())), preferred_element_type=F32)


def split(value):
    high = value.astype(BF16)
    return high, (value - high.astype(F32)).astype(BF16)


def place_kernel(
    expert_hbm, cloudy_hbm, state_hbm, out_ref,
    expert_ref, cloudy_ref, state_ref, chunk_ref, used_ref, sems
):
    networks, _, width = out_ref.shape
    blocks, levels, _ = state_ref.shape
    fetches = [
        pltpu.make_async_copy(state_hbm.at[:, block, :], state_ref.at[block], sems.at[block])
        for block in range(blocks)
    ]
    pairs = ((expert_hbm, expert_ref), (cloudy_hbm, cloudy_ref))
    early = [
        pltpu.make_async_copy(source, target, sems.at[blocks + i])
        for i, (source, target) in enumerate(pairs)
    ]
    for fetch in early + fetches:
        fetch.start()
    chunk_ref[...] = jnp.full((networks, levels, width), MARK, F32)
    for network in range(networks):
        used_ref[network] = 0
    for fetch in early:
        fetch.wait()
    lane = lax.broadcasted_iota(jnp.int32, (levels, CMAX), 1)
    spans = []
    for block in range(blocks):
        network = expert_ref[block]
        start = used_ref[network]
        end = start + cloudy_ref[block]
        used_ref[network] = end
        spans.append((network, start, end))
    for fetch in fetches:
        fetch.wait()
    for block, (network, start, end) in enumerate(spans):
        turned = pltpu.roll(0.5 * state_ref[block], lax.rem(start, CMAX), 1)
        here = (lane >= start) & (lane < end)
        pltpu.store(chunk_ref.at[network, :, :CMAX], turned, mask=here)
        pltpu.store(chunk_ref.at[network, :, CMAX:], turned, mask=lane + CMAX < end)
    out_ref[...] = chunk_ref[...].astype(BF16)


def place_blocks(experts, cloudy, state, networks):
    levels, blocks, width = state.shape
    return pl.pallas_call(
        place_kernel,
        in_specs=[HBM] * 3,
        out_specs=VMEM,
        out_shape=pltpu.HBM((networks, levels, CAP * CMAX), BF16),
        scratch_shapes=[
            pltpu.SMEM((blocks,), jnp.int32),
            pltpu.SMEM((blocks,), jnp.int32),
            pltpu.VMEM((blocks, levels, width), F32),
            pltpu.VMEM((networks, levels, CAP * CMAX), F32),
            pltpu.SMEM((networks,), jnp.int32),
            pltpu.SemaphoreType.DMA((blocks + 2,)),
        ],
        compiler_params=params(),
        name="place",
    )(*in_hbm(experts, cloudy, state))


def prepare_kernel(
    n_lon, order_ref, state_hbm, prev_hbm, high_hbm, low_hbm, in_hbm, mid_hbm, last_hbm,
    wave_hbm, analysis_hbm, rate_hbm, legendre_hbm,
    table_ref, out_ref, gain_ref, pull_ref, regain_ref, share_ref, first_ref, middle_ref, last_ref,
    state_ref, prev_ref, high_ref, low_ref, in_ref, mid_ref, wave_ref, analysis_ref, rate_ref, legendre_ref,
    sems
):
    levels, blocks, _ = state_ref.shape
    waves = order_ref.shape[0]
    pairs = (
        (mid_hbm, mid_ref), (in_hbm, in_ref), (last_hbm, last_ref),
        (high_hbm, high_ref), (state_hbm, state_ref), (prev_hbm, prev_ref), (low_hbm, low_ref),
        (wave_hbm, wave_ref), (analysis_hbm, analysis_ref), (rate_hbm, rate_ref),
        (legendre_hbm, legendre_ref),
    )
    fetches = [
        pltpu.make_async_copy(source, target, sems.at[i]) for i, (source, target) in enumerate(pairs)
    ]
    for fetch in fetches:
        fetch.start()
    for fetch in fetches[:4]:
        fetch.wait()
    side = waves
    diagonal = lax.broadcasted_iota(jnp.int32, (side, side), 0) == lax.broadcasted_iota(
        jnp.int32, (side, side), 1
    )
    half = jnp.where(diagonal, 0.5, 0.0).astype(BF16)
    for start in range(0, mid_ref.shape[1], side):
        rows = slice(start, start + side)
        middle_ref[rows, :] = dot_nt(half, mid_ref[:, rows]).astype(BF16)
        first_ref[rows, :] = (2.0 * dot_nt(half, in_ref[:, rows])).astype(BF16)
    for part in range(2):
        rows = slice(part * waves, (part + 1) * waves)
        table_ref[rows, :] = dot(order_ref[...], high_ref[rows, :]).astype(BF16)
    for fetch in fetches[4:]:
        fetch.wait()
    parts = [
        state_ref[:, block, :] + TIME_STEP * prev_ref[:, block, :] for block in range(blocks)
    ]
    forcing = jnp.concatenate(parts, axis=1)
    blank = jnp.zeros((LANES - levels, n_lon), F32)
    high, low = split(jnp.concatenate([forcing, blank], axis=0))
    both = dot_nt(high_ref[...], jnp.concatenate([high, low], axis=0))
    natural = both[:, :LANES] + (both[:, LANES:] + dot_nt(low_ref[...], high))
    natural = (natural * (1.0 / math.sqrt(n_lon))).astype(BF16)
    for part in range(2):
        rows = slice(part * waves, (part + 1) * waves)
        out_ref[rows, :] = dot(order_ref[...], natural[rows, :]).astype(BF16)

    networks, share, _ = share_ref.shape
    for network in range(networks):
        for half in range(CAP):
            part = legendre_ref[network, pl.ds(half, share, stride=CAP), :]
            share_ref[network, :, half * CMAX : (half + 1) * CMAX] = part.astype(BF16)
    lats = waves
    coeffs = gain_ref.shape[1]
    scale = 1.0 / (waves * (waves + 1.0))
    again = (n_lon / 2.0) / math.sqrt(waves) / math.sqrt(n_lon)
    wave = wave_ref[lax.axis_index("dyn") * networks + lax.axis_index("phys")]
    total = (wave + lax.broadcasted_iota(jnp.int32, (levels, coeffs), 1)).astype(F32)
    rate = jnp.concatenate([rate_ref[...], jnp.zeros((1, LANES - levels), F32)], axis=1)
    rate = jnp.broadcast_to(rate, (LANES, LANES)).T[:levels]
    rate = jnp.concatenate([rate, rate], axis=1)
    inverse = 1.0 / (1.0 + TIME_STEP * (total * (total + 1.0) * scale + rate))
    gap = jnp.zeros((LANES - levels, coeffs), F32)
    gains, pulls = [], []
    for part in range(2):
        halves = [analysis_ref[:, 2 * part + half, :] for half in range(2)]
        pulled = TIME_STEP * rate * jnp.concatenate(halves, axis=1) * inverse
        gains += [inverse * (1.0 / math.sqrt(lats) / math.sqrt(coeffs)), gap]
        pulls += [pulled * (1.0 / math.sqrt(coeffs)), gap]
    gain_ref[...] = jnp.concatenate(gains, axis=0)
    pull_ref[...] = jnp.concatenate(pulls, axis=0)
    real = jnp.where(wave == 0, 2.0 * again, again)
    imag = jnp.where(wave == 0, 0.0, again)
    lane = lax.broadcasted_iota(jnp.int32, (1, 2 * LANES), 1)
    regain_ref[...] = jnp.where(lane < LANES, real, imag)


def prepare(state, prev, order, high, low, w_in, w_mid, w_out, waves, analysis, rate, legendre):
    rows, n_lon = high.shape
    levels, hidden = w_in.shape
    coeffs = analysis.shape[1] * analysis.shape[2] // 2
    return pl.pallas_call(
        functools.partial(prepare_kernel, n_lon),
        in_specs=[VMEM] + [HBM] * 11,
        out_specs=[VMEM] * 9,
        out_shape=[
            pltpu.HBM((rows, n_lon), BF16),
            pltpu.HBM((rows, LANES), BF16),
            pltpu.HBM((2 * LANES, coeffs), F32),
            pltpu.HBM((2 * LANES, coeffs), F32),
            pltpu.HBM((1, 2 * LANES), F32),
            pltpu.HBM((legendre.shape[0], legendre.shape[1] // CAP, coeffs), BF16),
            jax.ShapeDtypeStruct((hidden, levels), BF16),
            jax.ShapeDtypeStruct((hidden, hidden), BF16),
            jax.ShapeDtypeStruct((levels, hidden), BF16),
        ],
        scratch_shapes=[
            pltpu.VMEM(state.shape, F32),
            pltpu.VMEM(prev.shape, F32),
            pltpu.VMEM(high.shape, BF16),
            pltpu.VMEM(low.shape, BF16),
            pltpu.VMEM(w_in.shape, BF16),
            pltpu.VMEM(w_mid.shape, BF16),
            pltpu.SMEM(waves.shape, jnp.int32),
            pltpu.VMEM(analysis.shape, F32),
            pltpu.VMEM(rate.shape, F32),
            pltpu.VMEM(legendre.shape, F32),
            pltpu.SemaphoreType.DMA((11,)),
        ],
        compiler_params=params(),
        cost_estimate=pl.CostEstimate(
            flops=4 * rows * n_lon * rows, bytes_accessed=12 << 20, transcendentals=0
        ),
        name="prepare",
    )(order, *in_hbm(state, prev, high, low, w_in, w_mid, w_out, waves, analysis, rate, legendre))


def silu(half):
    return (half + half * jnp.tanh(half)).astype(BF16)


def network_kernel(kept, x_ref, first_ref, middle_ref, last_ref, *refs):
    share_hbm, out_ref = refs[kept : kept + 2]
    packed_ref, done_ref, sems = refs[2 * kept + 2 :]
    senders, levels, _ = x_ref.shape
    share = share_hbm.shape[1]
    fetches = [
        pltpu.make_async_copy(refs[i], refs[kept + 2 + i], sems.at[i]) for i in range(kept)
    ] + [pltpu.make_async_copy(share_hbm, out_ref.at[:, :share, :], sems.at[kept])]
    for fetch in fetches:
        fetch.start()
    heads = [x_ref[sender, :16, :].astype(F32)[:1] for sender in range(senders)]
    marked = jnp.where(jnp.concatenate(heads, axis=0) < 0.1 * MARK, 1.0, 0.0)
    marked = marked[:, :CMAX] + marked[:, CMAX:]
    lane = lax.broadcasted_iota(jnp.int32, (levels, CMAX), 1)

    def tiles(start):
        first = start // CMAX
        return [pl.ds(pl.multiple_of((first + i) * CMAX, CMAX), CMAX) for i in range(3)]

    starts = [jnp.int32(0)]
    for sender in range(senders):
        count = jnp.sum(marked[sender : sender + 1]).astype(jnp.int32)
        starts.append(starts[-1] + count)
    for sender in range(senders):
        shift = lax.rem(starts[sender], CMAX)
        places = tiles(starts[sender])
        near = pltpu.roll(x_ref[sender, :, :CMAX].astype(F32), shift, 1)
        far = pltpu.roll(x_ref[sender, :, CMAX:].astype(F32), shift, 1)
        packed_ref[:, places[0]] = jnp.where(lane < shift, packed_ref[:, places[0]], near)
        packed_ref[:, places[1]] = jnp.where(lane < shift, near, far)
        packed_ref[:, places[2]] = far

    def run(start, width, step):
        place = pl.ds(pl.multiple_of(start, width), width)
        columns = packed_ref[:, place].astype(BF16)
        cuts = [slice(row, row + step) for row in range(0, middle_ref.shape[0], step)]
        one = jnp.concatenate([silu(dot(first_ref[cut, :], columns)) for cut in cuts], axis=0)
        two = jnp.concatenate([silu(dot(middle_ref[cut, :], one)) for cut in cuts], axis=0)
        done_ref[:, place] = dot(last_ref[...], two)

    def four(index, carry):
        for i in range(4):
            run((4 * index + i) * GROUP, GROUP, 256)
        return carry

    def single(index, carry):
        run(index * GROUP, GROUP, middle_ref.shape[0])
        return carry

    half = GROUP // 2
    halves = (starts[-1] + (half - 1)) // half
    groups = halves // 2
    lax.fori_loop(0, groups // 4, four, 0)
    lax.fori_loop(groups // 4 * 4, groups, single, 0)

    @pl.when(lax.rem(halves, 2) == 1)
    def _():
        run((halves - 1) * half, half, half)

    for sender in range(senders):
        shift = lax.rem(starts[sender], CMAX)
        back = lax.rem(CMAX - shift, CMAX)
        near, middle, far = (pltpu.roll(done_ref[:, place], back, 1) for place in tiles(starts[sender]))
        keep = lane < CMAX - shift
        out_ref[sender, share:, :CMAX] = jnp.where(keep, near, middle).astype(BF16)
        out_ref[sender, share:, CMAX:] = jnp.where(keep, middle, far).astype(BF16)
    for fetch in fetches:
        fetch.wait()


def network(arrived, first_w, middle_w, last_w, shares, *kept):
    senders, levels, width = arrived.shape
    share = shares.shape[1]
    hidden = last_w.shape[1]
    columns = -(-senders * width // GROUP) * GROUP + GROUP
    return pl.pallas_call(
        functools.partial(network_kernel, len(kept)),
        in_specs=[VMEM] * 4 + [HBM] * (1 + len(kept)),
        out_specs=[VMEM] * (1 + len(kept)),
        out_shape=[
            jax.ShapeDtypeStruct((senders, share + levels, width), BF16),
            *[pltpu.VMEM(array.shape, array.dtype) for array in kept],
        ],
        scratch_shapes=[
            pltpu.VMEM((levels, columns), F32),
            pltpu.VMEM((levels, columns), F32),
            pltpu.SemaphoreType.DMA((1 + len(kept),)),
        ],
        compiler_params=params(),
        cost_estimate=pl.CostEstimate(
            flops=senders * width * hidden * (hidden + 2 * 256),
            bytes_accessed=4 << 20,
            transcendentals=senders * width * hidden,
        ),
        name="network",
    )(arrived, first_w, middle_w, last_w, *in_hbm(*kept, shares))


def return_kernel(
    n_lon, returned_ref, table_ref, first_ref, expert_ref, cloudy_ref, tend_hbm, out_ref,
    tend_ref, used_ref, rows_ref, sems
):
    networks = returned_ref.shape[0]
    levels = tend_ref.shape[0]
    share = returned_ref.shape[1] - levels
    waves = first_ref.shape[0] // 2
    lanes = lax.broadcasted_iota(jnp.int32, (levels, CMAX), 1)
    for network in range(networks):
        used_ref[network] = 0
    spans = []
    for block in range(NB_ROW):
        network = expert_ref[block]
        start = used_ref[network]
        count = cloudy_ref[block]
        used_ref[network] = start + count
        spans.append((network, start, count))
    for block, (network, start, count) in enumerate(spans):
        back = lax.rem(2 * CMAX - start, CMAX)
        near = pltpu.roll(returned_ref[network, share:, :CMAX].astype(F32), back, 1)
        far = pltpu.roll(returned_ref[network, share:, CMAX:].astype(F32), back, 1)
        values = jnp.where(lanes < CMAX - start, near, far)
        kept = jnp.where(lanes < count, values, 0.0)
        tend_ref[:, block * CMAX : (block + 1) * CMAX] = kept.astype(BF16)
    leave = pltpu.make_async_copy(tend_ref, tend_hbm, sems.at[0])
    leave.start()
    out = dot_nt(table_ref[...], tend_ref[...]) * (TIME_STEP / math.sqrt(n_lon))
    out = jnp.concatenate([out, jnp.zeros((out.shape[0], LANES - levels), F32)], axis=1)
    for part in range(2):
        rows = slice(part * waves, (part + 1) * waves)
        rows_ref[pl.ds(part, waves, stride=4), :] = first_ref[rows, :].astype(F32)
        rows_ref[pl.ds(2 + part, waves, stride=4), :] = out[rows]
    out_ref[...] = rows_ref[...].astype(BF16)
    leave.wait()


def return_blocks(levels, returned, experts, cloudy, table, first):
    rows, n_lon = table.shape
    networks = returned.shape[0]
    return pl.pallas_call(
        functools.partial(return_kernel, n_lon),
        in_specs=[VMEM] * 3 + [SMEM] * 2,
        out_specs=[HBM, VMEM],
        out_shape=[
            pltpu.HBM((levels, n_lon), BF16),
            jax.ShapeDtypeStruct((2 * rows, LANES), BF16),
        ],
        scratch_shapes=[
            pltpu.VMEM((levels, n_lon), BF16),
            pltpu.SMEM((networks,), jnp.int32),
            pltpu.VMEM((2 * rows, LANES), F32),
            pltpu.SemaphoreType.DMA((1,)),
        ],
        compiler_params=params(),
        name="return",
    )(returned, table, first, experts, cloudy)


def solve_kernel(share, got_ref, own_ref, gain_ref, pull_ref, regain_ref, out_ref, rows_ref, turn_ref):
    networks = own_ref.shape[0]
    lats = networks * share
    rows_ref[...] = got_ref[...].astype(F32)
    parts = [rows_ref[pl.ds(part, lats, stride=4), :].astype(BF16) for part in range(4)]
    table = jnp.concatenate([own_ref[sender, :share, :] for sender in range(networks)], axis=0)
    gain = gain_ref[...]
    pull = pull_ref[...]
    regain = regain_ref[...]

    def there(value):
        both = dot_tn(jnp.concatenate(split(value), axis=1), table)
        return both[: 2 * LANES] + both[2 * LANES :]

    def back(value):
        both = dot_nt(table, jnp.concatenate(split(value), axis=0))
        return both[:, : 2 * LANES] + both[:, 2 * LANES :]

    spectral = dot_tn(jnp.concatenate(parts, axis=1), table)
    first = back(spectral[: 2 * LANES] * gain + pull)
    second = spectral[2 * LANES :] + there(first * regain)
    final = back(second * gain + pull)
    for part in range(2):
        turn_ref[pl.ds(part, lats, stride=2), :] = final[:, part * LANES : (part + 1) * LANES]
    out_ref[...] = turn_ref[...].astype(BF16)


def solve_twice(share, got, own, gain, pull, regain):
    rows = got.shape[0]
    return pl.pallas_call(
        functools.partial(solve_kernel, share),
        in_specs=[VMEM] * 5,
        out_specs=VMEM,
        out_shape=jax.ShapeDtypeStruct((rows // 2, LANES), BF16),
        scratch_shapes=[pltpu.VMEM((rows, LANES), F32), pltpu.VMEM((rows // 2, LANES), F32)],
        compiler_params=params(),
        name="solve",
    )(got, own, gain, pull, regain)


def synthesis_kernel(scale, home_ref, table_ref, out_hbm, rows_ref, out_ref, sems):
    levels, blocks, width = out_ref.shape
    waves = home_ref.shape[0] // 2
    rows_ref[...] = home_ref[...].astype(F32)
    parts = [rows_ref[pl.ds(part, waves, stride=2), :].astype(BF16) for part in range(2)]
    spectrum = jnp.concatenate(parts, axis=0).T
    cut = 4
    copies = []
    for start in range(0, blocks, cut):
        grid = dot(spectrum, table_ref[:, start * width : (start + cut) * width]) * scale
        for block in range(cut):
            out_ref[:, start + block, :] = grid[:levels, block * width : (block + 1) * width]
        place = slice(start, start + cut)
        copies.append(
            pltpu.make_async_copy(out_ref.at[:, place, :], out_hbm.at[:, place, :], sems.at[start // cut])
        )
        copies[-1].start()
    for copy in copies:
        copy.wait()


def synthesis(home, table, levels, scale):
    n_lon = table.shape[1]
    shape = (levels, NB_ROW, n_lon // NB_ROW)
    return pl.pallas_call(
        functools.partial(synthesis_kernel, scale),
        in_specs=[VMEM] * 2,
        out_specs=HBM,
        out_shape=pltpu.HBM(shape, F32),
        scratch_shapes=[
            pltpu.VMEM(home.shape, F32),
            pltpu.VMEM(shape, F32),
            pltpu.SemaphoreType.DMA((NB_ROW // 4,)),
        ],
        compiler_params=params(),
        name="synthesis",
    )(home, table)


def on_device(
    initial_state,
    prev_tendency,
    analysis,
    legendre,
    nudge_rate,
    band_waves,
    cloudy_count,
    expert_of,
    w_in,
    w_mid,
    w_out,
):
    levels, _, n_lon = initial_state.shape
    n_dyn = lax.axis_size("dyn")
    n_phys = lax.axis_size("phys")
    waves = band_waves.shape[0]
    coeffs = legendre.shape[3]
    lats = waves
    rows = 2 * waves
    state = initial_state.reshape(levels, NB_ROW, n_lon // NB_ROW)
    prev = prev_tendency.reshape(levels, NB_ROW, n_lon // NB_ROW)
    experts = expert_of[:, 0]

    share = lats // n_phys

    outgoing = place_blocks(experts, cloudy_count, state, n_phys)
    arrived = lax.all_to_all(outgoing, "phys", split_axis=0, concat_axis=0, tiled=True)

    high, low = (jnp.asarray(part) for part in wave_table(waves, n_lon))
    chunk_waves = band_waves.reshape(n_dyn, n_phys).T.reshape(waves, 1)
    order = (chunk_waves == jnp.arange(waves, dtype=jnp.int32)[None, :]).astype(BF16)
    table, first, gain, pull, regain, shares, first_w, middle_w, last_w = prepare(
        state,
        prev,
        order,
        high,
        low,
        w_in[0],
        w_mid[0],
        w_out[0],
        band_waves,
        analysis.reshape(levels, 2 * coeffs // LANES, LANES),
        nudge_rate[None, :],
        legendre.reshape(n_phys, share * CAP, coeffs // CAP),
    )
    arrived, first_w, middle_w, last_w, shares, *kept = lax.optimization_barrier(
        (arrived, first_w, middle_w, last_w, shares, table, first, gain, pull, regain)
    )
    computed, table, first, gain, pull, regain = network(
        arrived, first_w, middle_w, last_w, shares, *kept
    )
    returned = lax.all_to_all(computed, "phys", split_axis=0, concat_axis=0, tiled=True)

    tendency, sent = return_blocks(levels, returned, experts, cloudy_count, table, first)
    got = lax.all_to_all(
        sent.reshape(waves, 4, LANES), ORDER, split_axis=0, concat_axis=0, tiled=True
    )
    back = solve_twice(share, got.reshape(4 * lats, LANES), returned, gain, pull, regain)
    home = lax.all_to_all(
        back.reshape(lats, 2, LANES), ORDER, split_axis=0, concat_axis=0, tiled=True
    )
    final = synthesis(home.reshape(rows, LANES), table, levels, 1.0 / math.sqrt(waves))
    return (final.reshape(levels, 1, n_lon), tendency.reshape(levels, 1, n_lon))


def solution(mesh):
    in_specs = (
        P(None, ("dyn", "phys"), None),
        P(None, ("dyn", "phys"), None),
        P(None, None, ("dyn", "phys"), None),
        P("dyn", None, "phys", None),
        P(),
        P(),
        P(("dyn", "phys")),
        P(("dyn", "phys"), None),
        P("phys", None, None),
        P("phys", None, None),
        P("phys", None, None),
    )
    out_specs = (P(None, ("dyn", "phys"), None), P(None, ("dyn", "phys"), None))
    return jax.shard_map(
        on_device, mesh=mesh, in_specs=in_specs, out_specs=out_specs, check_vma=False
    )
```
